128 devices in a mesh: gz: 32 (over y, x_hi, z), vert: 4 (over x_lo, core).
Axes of the slice: x: 4 (x_hi: 2, x_lo: 2; x = x_hi * 2 + x_lo), y: 4, z: 4, core: 2. Of those that a mesh axis runs over, the one named last changes fastest.
Arguments:
- volume: bfloat16 [32, 131072], P('gz'), may hold values from -3 to 3
- dual: float32 [16, 64, 2048], P('vert', 'gz'), may hold values from -6 to 6
- counts: float32 [16, 64, 2048], P('vert', 'gz'), may hold values from 0 to 2.5
- cotangent: float32 [32, 131072], P('gz')
- dual_in: float32 [32, 3], replicated, may hold values from -3.5 to 3.5
- dual_bias: float32 [32], replicated, may hold values from -3 to 3
- dual_out: float32 [32], replicated, may hold values from -1 to 1
- primal_in: float32 [32, 2], replicated, may hold values from -4 to 4
- primal_bias: float32 [32], replicated, may hold values from -3 to 3
- primal_out: float32 [32], replicated, may hold values from -1 to 1
- blocks: bfloat16 [32, 4, 512, 128, 128], P('gz', 'vert'), may hold values from 0 to 0.079589844
- block_ray: int32 [32, 4, 512], P('gz', 'vert'), may hold values from 0 to 127
- block_vox: int32 [32, 4, 512], P('gz', 'vert'), may hold values from 0 to 3071
- block_count: int32 [32, 4], P('gz', 'vert'), may hold values from 128 to 512, as said below
Outputs:
- grad_volume: float32 [32, 131072], P('gz', 'vert')
- grad_dual: float32 [16, 64, 2048], P('vert', 'gz')
- grad_dual_in: float32 [32, 3], replicated
- grad_dual_bias: float32 [32], replicated
- grad_dual_out: float32 [32], replicated
- grad_primal_in: float32 [32, 2], replicated
- grad_primal_bias: float32 [32], replicated
- grad_primal_out: float32 [32], replicated
The draws below stay inside these ranges and needn't reach their ends.
Inputs may be any that keep to these rules, and one draw needn't show every extreme that they name: Blocks block_count to 511 of a device's list are padding; in every draw some device has all 512 blocks valid.
All inputs are finite; a program needn't handle non-finite values.
Results may differ from the reference program's by a relative error of at most 0.00033.
Values may be sent and summed in bfloat16 or wider, within the bound.
No kernel may reach another device: no remote copies, remote signals or barrier semaphores. Data moves between devices by JAX's collectives and lax.ppermute only.
A program may use at most 192 MiB of HBM per device.

```python
import math
import jax
import jax.numpy as jnp
from jax import lax

SZ = 1
TV = 128
TR = 128
NB = 512
VW = 4
DR = 2
CH = 32
NZ = 32
NV = 131072
DC = 2048
VIEWS = 16
NROWS = 64
RT = 128
KE = 3072
N_GZ = 32
N_VERT = 4


def draw_block_count(key, part):
    key = jax.random.fold_in(key, 11)
    first, second = jax.random.split(key)
    base_counts = jax.random.randint(first, (N_GZ * N_VERT,), NB // 4, NB + 1)
    full_device = jax.random.randint(second, (), 0, N_GZ * N_VERT)
    filled = jnp.where(jnp.arange(N_GZ * N_VERT) == full_device, NB, base_counts)
    return filled.reshape(N_GZ, N_VERT).astype(jnp.int32)


def draw_cotangent(key, part):
    key = jax.random.fold_in(key, 7)
    first = jax.random.fold_in(key, 0)
    steps = jnp.arange(NZ, dtype=jnp.float32) / max(NZ - 1, 1)
    rising = jnp.exp(math.log(3.0) * steps)[:, None]
    values = 1.0 + jax.random.normal(first, (NZ, NV), jnp.float32)
    return (values * rising).astype(jnp.float32)


def set_ends(drawn, rng, least, high):
    dims = drawn.shape
    spot = [jax.random.randint(jax.random.fold_in(rng, axis), (), 0, dims[axis]) for axis in range(len(dims))]
    drawn = drawn.at[tuple(spot)].set(least)
    longest = dims.index(max(dims))
    spot[longest] = (spot[longest] + 1) % dims[longest]
    return drawn.at[tuple(spot)].set(high)


def shard_levels(stream_key, extent, shards, least, high):
    gain = 1.0
    for axis_at, parts in shards:
        draws = jax.random.uniform(jax.random.fold_in(jax.random.fold_in(stream_key, 6), axis_at), (parts,), jnp.float32, least / len(shards), high / len(shards))
        gain = gain * jnp.repeat(jnp.exp(draws), extent[axis_at] // parts).reshape((-1,) + (1,) * (len(extent) - 1 - axis_at))
    return gain


def gaussian(rng, extent, deviation, reach, shards=(), held_as=jnp.bfloat16):
    loudness = shard_levels(rng, extent, shards, -0.22, 0.18) if shards else 1.0
    entries = jax.random.normal(rng, extent, jnp.float32) * deviation * loudness
    return jnp.minimum(jnp.maximum(entries, -reach), reach).astype(held_as)


def setup_inputs(seed: int = 0) -> dict:
    seeds = jax.random.split(jax.random.key(seed), 15)
    return {
        "volume": gaussian(seeds[0], (NZ, NV), 0.5, 3.0, ((0, 32),)),
        "dual": gaussian(seeds[1], (VIEWS, NROWS, DC), 1.0, 6.0, ((0, 4), (1, 32)), jnp.float32),
        "counts": jnp.clip(2.5 * jax.random.uniform(seeds[2], (VIEWS, NROWS, DC), jnp.float32) ** shard_levels(seeds[2], (VIEWS, NROWS, DC), ((0, 4), (1, 32)), -0.2, 0.2), 0.0, 2.5),
        "cotangent": draw_cotangent(jax.random.fold_in(seeds[14], 71), 0),
        "dual_in": gaussian(seeds[4], (CH, 3), 3 ** -0.5, 3.5, (), jnp.float32),
        "dual_bias": gaussian(seeds[5], (CH,), 0.5, 3.0, (), jnp.float32),
        "dual_out": gaussian(seeds[6], (CH,), CH ** -0.5, 1.0, (), jnp.float32),
        "primal_in": gaussian(seeds[7], (CH, 2), 2 ** -0.5, 4.0, (), jnp.float32),
        "primal_bias": gaussian(seeds[8], (CH,), 0.5, 3.0, (), jnp.float32),
        "primal_out": gaussian(seeds[9], (CH,), CH ** -0.5, 1.0, (), jnp.float32),
        "blocks": jnp.clip(0.079589844 * jax.random.uniform(seeds[10], (N_GZ, N_VERT, NB, TR, TV), jnp.float32) ** shard_levels(seeds[10], (N_GZ, N_VERT, NB, TR, TV), ((0, 32), (1, 4)), -0.2, 0.2), 0.0, 0.079589844).astype(jnp.bfloat16),
        "block_ray": set_ends(jax.random.randint(seeds[11], (N_GZ, N_VERT, NB), 0, RT), jax.random.fold_in(seeds[11], 1), 0, RT - 1).astype(jnp.int32),
        "block_vox": set_ends(jax.random.randint(seeds[12], (N_GZ, N_VERT, NB), 0, KE), jax.random.fold_in(seeds[12], 1), 0, KE - 1).astype(jnp.int32),
        "block_count": draw_block_count(jax.random.fold_in(seeds[14], 71), 0),
    }


def to_rays(sinogram):
    shaped = sinogram.reshape(N_VERT, VW, N_GZ, DR, DC).transpose(2, 0, 1, 3, 4)
    return shaped.reshape(N_GZ, N_VERT, RT, TR)


def from_rays(values):
    shaped = values.reshape(N_GZ, N_VERT, VW, DR, DC).transpose(1, 2, 0, 3, 4)
    return shaped.reshape(VIEWS, NROWS, DC)


def dsilu(hidden, gate_vals):
    return gate_vals * (1.0 + hidden * (1.0 - gate_vals))


def reference(volume, dual, counts, cotangent, dual_in, dual_bias, dual_out, primal_in, primal_bias, primal_out, blocks, block_ray, block_vox, block_count):
    valid_rows = (jnp.arange(NB)[None, None, :] < block_count[:, :, None]).astype(jnp.float32)
    vert_rows = jnp.broadcast_to(jnp.arange(N_VERT, dtype=jnp.int32)[:, None], (N_VERT, NB))
    slab_ids = jnp.arange(N_GZ, dtype=jnp.int32)
    highest = lax.Precision.HIGHEST

    def forward_project(field):
        padded = jnp.pad(field, ((1, 1), (0, 0)))

        def one_slab(slab_id):
            extended = lax.dynamic_slice_in_dim(padded, slab_id * SZ, SZ + 2, 0)
            extended = extended.reshape(KE, TV).astype(jnp.float32)
            picked = extended[block_vox[slab_id]]
            products = jnp.einsum("vbtk,vbk->vbt", blocks[slab_id].astype(jnp.float32), picked)
            products = products * valid_rows[slab_id][..., None]
            return jnp.zeros((N_VERT, RT, TR), jnp.float32).at[vert_rows, block_ray[slab_id]].add(products)

        return from_rays(lax.map(one_slab, slab_ids))

    def back_project(sinogram):
        rays_all = to_rays(sinogram).astype(jnp.float32)

        def one_slab(slab_id):
            picked = rays_all[slab_id][vert_rows, block_ray[slab_id]]
            partial_cols = jnp.einsum("vbtk,vbt->vbk", blocks[slab_id].astype(jnp.float32), picked)
            partial_cols = partial_cols * valid_rows[slab_id][..., None]
            summed = jnp.zeros((KE, TV), jnp.float32).at[block_vox[slab_id]].add(partial_cols)
            return summed.reshape(SZ + 2, NV)

        extended = lax.map(one_slab, slab_ids)
        middle = extended[:, 1:SZ + 1].reshape(NZ, NV)
        middle = middle.at[jnp.arange(1, N_GZ) * SZ - 1].add(extended[1:, 0])
        middle = middle.at[jnp.arange(0, N_GZ - 1) * SZ + SZ].add(extended[:-1, SZ + 1])
        return middle

    sinogram = forward_project(volume)
    expected = jnp.exp(-sinogram)
    inputs = jnp.stack([dual.reshape(-1), sinogram.reshape(-1), (expected - counts).reshape(-1)])
    hidden_dual = jnp.dot(dual_in, inputs, precision=highest) + dual_bias[:, None]
    gate_dual = jax.nn.sigmoid(hidden_dual)
    act_dual = hidden_dual * gate_dual
    new_dual = (dual.reshape(-1) + jnp.dot(dual_out, act_dual, precision=highest)).astype(jnp.bfloat16)
    backproj = back_project(new_dual.reshape(VIEWS, NROWS, DC))

    stacked = jnp.stack([volume.astype(jnp.float32).reshape(-1), backproj.reshape(-1)])
    hidden_primal = jnp.dot(primal_in, stacked, precision=highest) + primal_bias[:, None]
    gate_primal = jax.nn.sigmoid(hidden_primal)
    act_primal = hidden_primal * gate_primal
    flat_cot = cotangent.reshape(-1)
    error_primal = primal_out[:, None] * flat_cot[None, :] * dsilu(hidden_primal, gate_primal)
    pulled = jnp.dot(primal_in.T, error_primal, precision=highest)
    back_grad = pulled[1].reshape(NZ, NV).astype(jnp.bfloat16)

    dual_grad_in = forward_project(back_grad).reshape(-1)
    error_dual = dual_out[:, None] * dual_grad_in[None, :] * dsilu(hidden_dual, gate_dual)
    pulled_dual = jnp.dot(dual_in.T, error_dual, precision=highest)
    grad_dual = (dual_grad_in + pulled_dual[0]).reshape(VIEWS, NROWS, DC)
    sino_grad = (pulled_dual[1] - expected.reshape(-1) * pulled_dual[2]).astype(jnp.bfloat16)
    direct = (flat_cot + pulled[0]).reshape(NZ, NV)
    grad_volume = back_project(sino_grad.reshape(VIEWS, NROWS, DC)) + direct

    ray_total = 1.0 / (VIEWS * NROWS * DC)
    vox_total = 1.0 / (NZ * NV)
    grad_dual_in = jnp.dot(error_dual, inputs.T, precision=highest) * ray_total
    grad_dual_bias = jnp.sum(error_dual, axis=1) * ray_total
    grad_dual_out = jnp.sum(act_dual * dual_grad_in[None, :], axis=1) * ray_total
    grad_primal_in = jnp.dot(error_primal, stacked.T, precision=highest) * vox_total
    grad_primal_bias = jnp.sum(error_primal, axis=1) * vox_total
    grad_primal_out = jnp.sum(act_primal * flat_cot[None, :], axis=1) * vox_total
    return (grad_volume, grad_dual, grad_dual_in, grad_dual_bias, grad_dual_out, grad_primal_in, grad_primal_bias, grad_primal_out)
```

```python
import functools

import jax
import jax.numpy as jnp
from jax import lax
from jax.experimental import pallas as pl
from jax.experimental.pallas import tpu as pltpu
from jax.sharding import PartitionSpec as P

F32 = jnp.float32
BF16 = jnp.bfloat16
VMEM = pl.BlockSpec(memory_space=pltpu.VMEM)
SMEM = pl.BlockSpec(memory_space=pltpu.SMEM)
HBM = pl.BlockSpec(memory_space=pl.ANY)
NT = (((1,), (1,)), ((), ()))
GROUP = 16
CHUNKS = 16
MIB = 1024 * 1024


def sigmoid(x):
    return 0.5 * jnp.tanh(0.5 * x) + 0.5


def in_three(x):
    high = x.astype(BF16)
    rest = x - high.astype(F32)
    middle = rest.astype(BF16)
    return high, middle, (rest - middle.astype(F32)).astype(BF16)


def dot(a, b):
    return jnp.dot(a, b, preferred_element_type=F32)


def load_blocks(blocks, held, sems):
    per = held.shape[0] // CHUNKS
    copies = [
        pltpu.make_async_copy(
            blocks.at[pl.ds(i * per, per), :], held.at[pl.ds(i * per, per), :], sems.at[i]
        )
        for i in range(CHUNKS)
    ]
    for copy in copies:
        copy.start()
    return copies


def gather_tiles(vox, ext, picked):
    def body(i, carry):
        for j in range(16):
            b = i * 16 + j
            picked[pl.ds(b, 1), :] = ext[pl.ds(vox[b], 1), :]
        return carry

    lax.fori_loop(0, picked.shape[0] // 16, body, 0)


def project(copies, held, picked, products):
    count, size = picked.shape
    row = lax.broadcasted_iota(jnp.int32, (GROUP, size), 0)
    per = count // CHUNKS // GROUP
    for i, copy in enumerate(copies):
        copy.wait()
        for g in range(i * per, (i + 1) * per):
            x = picked[g * GROUP : (g + 1) * GROUP, :].astype(BF16)
            full = lax.dot_general(
                x,
                held[g * GROUP * size : (g + 1) * GROUP * size, :],
                NT,
                preferred_element_type=F32,
            )
            y = full[:, :size]
            for b in range(1, GROUP):
                y = jnp.where(row == b, full[:, b * size : (b + 1) * size], y)
            products[g * GROUP : (g + 1) * GROUP, :] = y


def spread(held, picked, out):
    count, size = out.shape
    row = lax.broadcasted_iota(jnp.int32, (GROUP, size), 0)
    for g in range(count // GROUP):
        s = picked[g * GROUP : (g + 1) * GROUP, :]
        diagonal = jnp.concatenate(
            [jnp.where(row == b, s, 0.0).astype(BF16) for b in range(GROUP)], axis=1
        )
        out[g * GROUP : (g + 1) * GROUP, :] = dot(
            diagonal, held[g * GROUP * size : (g + 1) * GROUP * size, :]
        )


def ray_choice(ray, count, tiles):
    shape = (tiles, ray.shape[1])
    tile = lax.broadcasted_iota(jnp.int32, shape, 0)
    block = lax.broadcasted_iota(jnp.int32, shape, 1)
    return jnp.where((ray[...] == tile) & (block < count[0]), 1.0, 0.0)


def add_rays(chosen, products):
    chosen = chosen.astype(BF16)
    high, middle, low = in_three(products[...])
    return dot(chosen, high) + dot(chosen, middle) + dot(chosen, low)


def forward_kernel(
    count, vox, ray, low, own, high, blocks, dual, counts, w_in, w_bias, w_out,
    sinogram, partial, ext, picked, products, held, sems,
):
    copies = load_blocks(blocks, held, sems)
    rows = own.shape[0]
    for i, field in enumerate((low, own, high)):
        ext[i * rows : (i + 1) * rows, :] = field[...].astype(F32)
    gather_tiles(vox, ext, picked)
    project(copies, held, picked, products)
    tiles, size = dual.shape
    chosen = ray_choice(ray, count, tiles)
    sinogram[...] = add_rays(chosen, products)
    part = 64
    fresh = []
    for start in range(0, tiles, part):
        rows = slice(start, start + part)
        d = dual[rows, :]
        s = sinogram[rows, :]
        r = jnp.exp(-s) - counts[rows, :]

        def channel(c, total):
            h = w_in[c, 0] * d + w_in[c, 1] * s + w_in[c, 2] * r + w_bias[c]
            return total + w_out[c] * (h * sigmoid(h))

        fresh.append(lax.fori_loop(0, w_bias.shape[0], channel, jnp.zeros_like(d), unroll=4) + d)
    new_dual = jnp.concatenate(fresh, axis=0).astype(BF16)
    picked[...] = dot(chosen.T.astype(BF16), new_dual)
    spread(held, picked, partial)


def backward_kernel(
    me, count, vox, ray, low, high, own, near1, own1, near2, own2, near3, own3,
    blocks, dual, counts, sinogram, w_in, w_bias, w_out,
    grad_dual, partial, sums, ext, picked, products, held, totals, sems,
):
    copies = load_blocks(blocks, held, sems)
    rows = own.shape[0]
    pieces = [
        (low, own, high),
        (near1.at[0], own1, near1.at[1]),
        (near2.at[0], own2, near2.at[1]),
        (near3.at[0], own3, near3.at[1]),
    ]
    for d, fields in enumerate(pieces):
        for i, field in enumerate(fields):
            at = pl.multiple_of((i * len(pieces) + (me[0] ^ d)) * rows, rows)
            ext[pl.ds(at, rows), :] = field[...].astype(F32)
    gather_tiles(vox, ext, picked)
    project(copies, held, picked, products)
    tiles, size = dual.shape
    chosen = ray_choice(ray, count, tiles)
    products[0:tiles, :] = add_rays(chosen, products)
    totals[...] = jnp.zeros_like(totals)
    part = 32
    grads = []
    for start in range(0, tiles, part):
        rows = slice(start, start + part)
        d = dual[rows, :]
        s = sinogram[rows, :]
        e = jnp.exp(-s)
        r = e - counts[rows, :]
        g = products[rows, :]

        def channel(c, carry):
            p0, p1, p2 = carry
            w0, w1, w2 = w_in[c, 0], w_in[c, 1], w_in[c, 2]
            h = w0 * d + w1 * s + w2 * r + w_bias[c]
            gate = sigmoid(h)
            act = h * gate
            err = (w_out[c] * g) * (gate + act * (1.0 - gate))

            def fold(x):
                return jnp.sum(x.reshape(part // 8, 8, size), axis=0)

            totals[c, 0] += fold(err * d)
            totals[c, 1] += fold(err * s)
            totals[c, 2] += fold(err * r)
            totals[c, 3] += fold(err)
            totals[c, 4] += fold(act * g)
            return p0 + w0 * err, p1 + w1 * err, p2 + w2 * err

        zero = jnp.zeros_like(d)
        p0, p1, p2 = lax.fori_loop(0, w_bias.shape[0], channel, (zero, zero, zero), unroll=2)
        grad_dual[rows, :] = g + p0
        grads.append(p1 - e * p2)
    sino_grad = jnp.concatenate(grads, axis=0).astype(BF16)
    picked[...] = dot(chosen.T.astype(BF16), sino_grad)
    spread(held, picked, partial)
    channels = w_bias.shape[0]
    for k in range(5):
        lanes = jnp.sum(totals[:, k], axis=1)
        sums[k : k + 1, :] = jnp.sum(lanes.T, axis=0, keepdims=True)


def place(vox, values, first, rows):
    tile = lax.broadcasted_iota(jnp.int32, (rows, vox.shape[1]), 0)
    chosen = jnp.where(vox[...] - first == tile, 1.0, 0.0).astype(BF16)
    size = values.shape[1] // 3
    out = dot(chosen, values)
    return out[:, :size] + out[:, size : 2 * size] + out[:, 2 * size :]


def own_kernel(me, vox, values, out):
    groups, rows, _ = out.shape
    parts = jnp.concatenate(in_three(values[...]), axis=1)
    for d in range(groups):
        first = (groups + (me[0] ^ d)) * rows
        out[d] = place(vox, parts, first, rows)


def fold_kernel(me, held, vox_low, from_low, vox_high, from_high, *outs):
    groups, rows, _ = held.shape
    low = jnp.concatenate(in_three(from_low[...]), axis=1)
    high = jnp.concatenate(in_three(from_high[...]), axis=1)
    for d in range(groups):
        first = (me[0] ^ d) * rows
        outs[d][...] = (
            held[d]
            + place(vox_low, low, 2 * groups * rows + first, rows)
            + place(vox_high, high, first, rows)
        )


def primal_kernel(
    me, own, peer1, peer2, peer3, volume, cotangent, w_in, w_bias, w_out,
    back_grad, direct, sums, totals,
):
    rows, size = own.shape
    base = me[0] * rows
    totals[...] = jnp.zeros_like(totals)
    part = 64

    def chunk(i, done):
        at = pl.ds(pl.multiple_of(i * part, part), part)
        there = pl.ds(pl.multiple_of(base + i * part, part), part)
        b = own[at, :] + peer1[at, :] + peer2[at, :] + peer3[at, :]
        v = volume[there, :].astype(F32)
        t = cotangent[there, :]

        def channel(c, carry):
            p0, p1 = carry
            w0, w1 = w_in[c, 0], w_in[c, 1]
            h = w0 * v + w1 * b + w_bias[c]
            gate = sigmoid(h)
            act = h * gate
            err = (w_out[c] * t) * (gate + act * (1.0 - gate))

            def fold(x):
                return jnp.sum(x.reshape(part // 8, 8, size), axis=0)

            totals[c, 0] += fold(err * v)
            totals[c, 1] += fold(err * b)
            totals[c, 2] += fold(err)
            totals[c, 3] += fold(act * t)
            return p0 + w0 * err, p1 + w1 * err

        zero = jnp.zeros_like(t)
        p0, p1 = lax.fori_loop(0, w_bias.shape[0], channel, (zero, zero), unroll=2)
        back_grad[at, :] = p1.astype(BF16)
        direct[at, :] = t + p0
        return done

    lax.fori_loop(0, rows // part, chunk, 0)
    for k in range(4):
        lanes = jnp.sum(totals[:, k], axis=1)
        sums[k : k + 1, :] = jnp.sum(lanes.T, axis=0, keepdims=True)


def call(body, out_shapes, specs, args, scratch=(), flops=0, bytes_moved=0, limit=56):
    return pl.pallas_call(
        body,
        out_shape=out_shapes,
        in_specs=specs,
        out_specs=[VMEM] * len(out_shapes),
        scratch_shapes=list(scratch),
        compiler_params=pltpu.CompilerParams(vmem_limit_bytes=limit * MIB),
        cost_estimate=pl.CostEstimate(
            flops=flops, bytes_accessed=bytes_moved, transcendentals=0
        ),
    )(*args)


def local(
    volume, dual, counts, cotangent, dual_in, dual_bias, dual_out,
    primal_in, primal_bias, primal_out, blocks, block_ray, block_vox, block_count,
):
    listed, tr, tv = blocks.shape[2:]
    voxels = volume.shape[1]
    tiles = voxels // tv
    views, det_rows, cols = dual.shape
    col_tiles = cols // tr
    ray_tiles = dual.size // tr
    channels = dual_bias.shape[0]
    groups = lax.axis_size("vert")
    slabs = lax.axis_size("gz")
    rows = tiles // groups
    me = lax.axis_index("vert").reshape(1).astype(jnp.int32)
    ray_total = 1.0 / (dual.size * slabs * groups)
    vox_total = 1.0 / (voxels * slabs)
    up = [(i, i + 1) for i in range(slabs - 1)]
    down = [(i + 1, i) for i in range(slabs - 1)]

    def shape(*dims, dtype=F32):
        return jax.ShapeDtypeStruct(dims, dtype)

    def beside(x):
        return lax.ppermute(x, "gz", up), lax.ppermute(x, "gz", down)

    def peer(x, d):
        return lax.ppermute(x, "vert", [(i, i ^ d) for i in range(groups)])

    def to_tiles(x):
        x = x.reshape(views, det_rows, col_tiles, tr).transpose(0, 2, 1, 3)
        return x.reshape(ray_tiles, tr)

    def from_tiles(x):
        x = x.reshape(views, col_tiles, det_rows, tr).transpose(0, 2, 1, 3)
        return x.reshape(views, det_rows, cols)

    matrix = blocks.reshape(listed * tr, tv)
    count = block_count.reshape(1)
    vox = block_vox.reshape(listed)
    ray = block_ray.reshape(1, listed)
    per_view = det_rows * col_tiles
    ray = (ray // per_view) * per_view + (ray % col_tiles) * det_rows + (ray // col_tiles) % det_rows
    listed_at = lax.broadcasted_iota(jnp.int32, (1, listed), 1)
    vox_row = jnp.where(listed_at < count[0], vox[None, :], -1)
    field = volume.reshape(tiles, tv)
    cot = cotangent.reshape(tiles, tv)
    dual_tiles = to_tiles(dual)
    count_tiles = to_tiles(counts)

    big = [
        pltpu.VMEM((3 * tiles, tv), F32),
        pltpu.VMEM((listed, tv), F32),
        pltpu.VMEM((listed, tr), F32),
        pltpu.VMEM((listed * tr, tv), BF16),
    ]
    low, high = beside(field)
    vox_low, vox_high = beside(vox_row)
    sinogram, partial = call(
        forward_kernel,
        [shape(ray_tiles, tr), shape(listed, tv)],
        [SMEM, SMEM, VMEM, VMEM, VMEM, VMEM, HBM, VMEM, VMEM, SMEM, SMEM, SMEM],
        (count, vox, ray, low, field, high, matrix, dual_tiles, count_tiles,
         dual_in, dual_bias, dual_out),
        big + [pltpu.SemaphoreType.DMA((CHUNKS,))],
        bytes_moved=3 * matrix.size,
    )

    def reduced(partial):
        from_low, from_high = beside(partial)
        held = call(
            own_kernel,
            [shape(groups, rows, tv)],
            [SMEM, VMEM, VMEM],
            (me, vox_row, partial),
            bytes_moved=4 * MIB,
            limit=32,
        )[0]
        parts = call(
            fold_kernel,
            [shape(rows, tv)] * groups,
            [SMEM] + [VMEM] * 5,
            (me, held, vox_low, from_low, vox_high, from_high),
            bytes_moved=8 * MIB,
            limit=32,
        )
        return [parts[0]] + [peer(parts[d], d) for d in range(1, groups)]

    pieces = reduced(partial)
    back_grad, direct, primal_sums = call(
        primal_kernel,
        [shape(rows, tv, dtype=BF16), shape(rows, tv), shape(4, channels)],
        [SMEM] + [VMEM] * 6 + [SMEM] * 3,
        (me, *pieces, field, cot, primal_in, primal_bias, primal_out),
        [pltpu.VMEM((channels, 4, 8, tv), F32)],
        bytes_moved=16 * MIB,
        limit=32,
    )
    near_low, near_high = beside(back_grad)
    near = jnp.stack([near_low, near_high])
    fields = [near_low, near_high, back_grad]
    for d in range(1, groups):
        fields += [peer(near, d), peer(back_grad, d)]
    grad_dual, partial, dual_sums = call(
        backward_kernel,
        [shape(ray_tiles, tr), shape(listed, tv), shape(5, channels)],
        [SMEM] * 3 + [VMEM] * 10 + [HBM] + [VMEM] * 3 + [SMEM] * 3,
        (me, count, vox, ray, *fields, matrix, dual_tiles, count_tiles, sinogram,
         dual_in, dual_bias, dual_out),
        big + [pltpu.VMEM((channels, 5, 8, tr), F32), pltpu.SemaphoreType.DMA((CHUNKS,))],
        bytes_moved=3 * matrix.size,
    )
    pieces = reduced(partial)
    grad_volume = pieces[0] + pieces[1] + pieces[2] + pieces[3] + direct

    sums = jnp.concatenate([dual_sums * ray_total, primal_sums * vox_total])
    sent = jnp.broadcast_to(sums[None], (slabs * groups, *sums.shape))
    summed = jnp.sum(lax.all_to_all(sent, ("gz", "vert"), 0, 0), axis=0)
    return (
        grad_volume.reshape(1, rows * tv),
        from_tiles(grad_dual),
        summed[0:3].T,
        summed[3],
        summed[4],
        summed[5:7].T,
        summed[7],
        summed[8],
    )


def solution(mesh):
    in_specs = (
        P("gz", None),
        P("vert", "gz", None),
        P("vert", "gz", None),
        P("gz", None),
        P(), P(), P(), P(), P(), P(),
        P("gz", "vert", None, None, None),
        P("gz", "vert", None),
        P("gz", "vert", None),
        P("gz", "vert"),
    )
    out_specs = (P("gz", "vert"), P("vert", "gz", None), P(), P(), P(), P(), P(), P())
    return jax.shard_map(local, mesh=mesh, in_specs=in_specs, out_specs=out_specs, check_vma=False)
```

```python
import functools

import jax
import jax.numpy as jnp
from jax import lax
from jax.experimental import pallas as pl
from jax.experimental.pallas import tpu as pltpu
from jax.sharding import PartitionSpec as P

F32 = jnp.float32
BF16 = jnp.bfloat16
VMEM = pl.BlockSpec(memory_space=pltpu.VMEM)
SMEM = pl.BlockSpec(memory_space=pltpu.SMEM)
HBM = pl.BlockSpec(memory_space=pl.ANY)
NT = (((1,), (1,)), ((), ()))
GROUP = 16
CHUNKS = 16
MIB = 1024 * 1024


def sigmoid(x):
    return 0.5 * jnp.tanh(0.5 * x) + 0.5


def in_three(x):
    high = x.astype(BF16)
    rest = x - high.astype(F32)
    middle = rest.astype(BF16)
    return high, middle, (rest - middle.astype(F32)).astype(BF16)


def dot(a, b):
    return jnp.dot(a, b, preferred_element_type=F32)


def hold_kernel(blocks, _, held, sems):
    per = held.shape[0] // CHUNKS
    copies = []
    for i in range(CHUNKS):
        rows = pl.ds(i * per, per)
        copies.append(pltpu.make_async_copy(blocks.at[rows, :], held.at[rows, :], sems.at[i]))
        copies[i].start()
    for copy in copies:
        copy.wait()


def gather_tiles(vox, ext, picked):
    def body(i, carry):
        for j in range(16):
            b = i * 16 + j
            picked[pl.ds(b, 1), :] = ext[pl.ds(vox[b], 1), :]
        return carry

    lax.fori_loop(0, picked.shape[0] // 16, body, 0)


def project(held, picked, products):
    count, size = picked.shape
    row = lax.broadcasted_iota(jnp.int32, (GROUP, size), 0)
    for g in range(count // GROUP):
        x = picked[g * GROUP : (g + 1) * GROUP, :].astype(BF16)
        full = lax.dot_general(
            x,
            held[g * GROUP * size : (g + 1) * GROUP * size, :],
            NT,
            preferred_element_type=F32,
        )
        y = full[:, :size]
        for b in range(1, GROUP):
            y = jnp.where(row == b, full[:, b * size : (b + 1) * size], y)
        products[g * GROUP : (g + 1) * GROUP, :] = y


def spread(held, picked, out):
    count, size = picked.shape
    row = lax.broadcasted_iota(jnp.int32, (GROUP, size), 0)
    for g in range(count // GROUP):
        s = picked[g * GROUP : (g + 1) * GROUP, :]
        diagonal = jnp.concatenate(
            [jnp.where(row == b, s, 0.0).astype(BF16) for b in range(GROUP)], axis=1
        )
        out[g * GROUP : (g + 1) * GROUP, :] = dot(
            diagonal, held[g * GROUP * size : (g + 1) * GROUP * size, :]
        )


def mark_tiles(tile, out):
    count, size = tile.shape[1], out.shape[1]
    parts = [tile[:, i * size : (i + 1) * size] for i in range(count // size)]
    rows = jnp.concatenate(parts + parts, axis=0)
    out[count : count + 8, :] = rows.astype(F32)


def ray_choice(ray, count, tiles):
    shape = (tiles, ray.shape[1])
    tile = lax.broadcasted_iota(jnp.int32, shape, 0)
    block = lax.broadcasted_iota(jnp.int32, shape, 1)
    return jnp.where((ray[...] == tile) & (block < count[0]), 1.0, 0.0)


def add_rays(chosen, products):
    chosen = chosen.astype(BF16)
    high, middle, low = in_three(products[...])
    return dot(chosen, high) + dot(chosen, middle) + dot(chosen, low)


def forward_kernel(
    count, vox, tile, ray, low, own, high, blocks, dual, counts, w_in, w_bias, w_out,
    sinogram, partial, ext, picked, products,
):
    rows = own.shape[0]
    for i, field in enumerate((low, own, high)):
        ext[i * rows : (i + 1) * rows, :] = field[...].astype(F32)
    gather_tiles(vox, ext, picked)
    project(blocks, picked, products)
    tiles, size = dual.shape
    chosen = ray_choice(ray, count, tiles)
    sinogram[...] = add_rays(chosen, products)
    part = 64
    fresh = []
    for start in range(0, tiles, part):
        rows = slice(start, start + part)
        d = dual[rows, :]
        s = sinogram[rows, :]
        r = jnp.exp(-s) - counts[rows, :]

        def channel(c, total):
            h = w_in[c, 0] * d + w_in[c, 1] * s + w_in[c, 2] * r + w_bias[c]
            return total + w_out[c] * (h * sigmoid(h))

        fresh.append(lax.fori_loop(0, w_bias.shape[0], channel, jnp.zeros_like(d), unroll=4) + d)
    new_dual = jnp.concatenate(fresh, axis=0).astype(BF16)
    picked[...] = dot(chosen.T.astype(BF16), new_dual)
    spread(blocks, picked, partial)
    mark_tiles(tile, partial)


def backward_kernel(
    me, count, vox, tile, ray, low, high, own, near1, own1, near2, own2, near3, own3,
    blocks, dual, counts, sinogram, w_in, w_bias, w_out,
    grad_dual, partial, sums, ext, picked, products, totals,
):
    rows = own.shape[0]
    pieces = [
        (low, own, high),
        (near1.at[0], own1, near1.at[1]),
        (near2.at[0], own2, near2.at[1]),
        (near3.at[0], own3, near3.at[1]),
    ]
    for d, fields in enumerate(pieces):
        for i, field in enumerate(fields):
            at = pl.multiple_of((i * len(pieces) + (me[0] ^ d)) * rows, rows)
            ext[pl.ds(at, rows), :] = field[...].astype(F32)
    gather_tiles(vox, ext, picked)
    project(blocks, picked, products)
    tiles, size = dual.shape
    chosen = ray_choice(ray, count, tiles)
    products[0:tiles, :] = add_rays(chosen, products)
    totals[...] = jnp.zeros_like(totals)
    part = 32
    grads = []
    for start in range(0, tiles, part):
        rows = slice(start, start + part)
        d = dual[rows, :]
        s = sinogram[rows, :]
        e = jnp.exp(-s)
        r = e - counts[rows, :]
        g = products[rows, :]

        def channel(c, carry):
            p0, p1, p2 = carry
            w0, w1, w2 = w_in[c, 0], w_in[c, 1], w_in[c, 2]
            h = w0 * d + w1 * s + w2 * r + w_bias[c]
            gate = sigmoid(h)
            act = h * gate
            err = (w_out[c] * g) * (gate + act * (1.0 - gate))

            def fold(x):
                return jnp.sum(x.reshape(part // 8, 8, size), axis=0)

            totals[c, 0] += fold(err * d)
            totals[c, 1] += fold(err * s)
            totals[c, 2] += fold(err * r)
            totals[c, 3] += fold(err)
            totals[c, 4] += fold(act * g)
            return p0 + w0 * err, p1 + w1 * err, p2 + w2 * err

        zero = jnp.zeros_like(d)
        p0, p1, p2 = lax.fori_loop(0, w_bias.shape[0], channel, (zero, zero, zero), unroll=2)
        grad_dual[rows, :] = g + p0
        grads.append(p1 - e * p2)
    sino_grad = jnp.concatenate(grads, axis=0).astype(BF16)
    picked[...] = dot(chosen.T.astype(BF16), sino_grad)
    spread(blocks, picked, partial)
    mark_tiles(tile, partial)
    channels = w_bias.shape[0]
    for k in range(5):
        lanes = jnp.sum(totals[:, k], axis=1)
        sums[k : k + 1, :] = jnp.sum(lanes.T, axis=0, keepdims=True)


def split_marked(marked):
    count = marked.shape[0] - 8
    marks = marked[count:, :].astype(jnp.int32)
    vox = jnp.concatenate([marks[i : i + 1, :] for i in range(count // marked.shape[1])], axis=1)
    return vox, jnp.concatenate(in_three(marked[:count, :]), axis=1)


def place(vox, values, first, rows):
    tile = lax.broadcasted_iota(jnp.int32, (rows, vox.shape[1]), 0)
    chosen = jnp.where(vox - first == tile, 1.0, 0.0).astype(BF16)
    size = values.shape[1] // 3
    out = dot(chosen, values)
    return out[:, :size] + out[:, size : 2 * size] + out[:, 2 * size :]


def own_kernel(me, partial, sums, out, sums_out):
    groups, rows, _ = out.shape
    sums_out[...] = sums[...]
    vox, values = split_marked(partial)
    for d in range(groups):
        out[d] = place(vox, values, (groups + (me[0] ^ d)) * rows, rows)


def fold_kernel(me, held, from_low, from_high, *outs):
    groups, rows, _ = held.shape
    vox_low, low = split_marked(from_low)
    vox_high, high = split_marked(from_high)
    for d in range(groups):
        first = (me[0] ^ d) * rows
        outs[d][...] = (
            held[d]
            + place(vox_low, low, 2 * groups * rows + first, rows)
            + place(vox_high, high, first, rows)
        )


def primal_kernel(
    me, own, peer1, peer2, peer3, volume, cotangent, w_in, w_bias, w_out,
    back_grad, direct, sums, totals,
):
    rows, size = own.shape
    base = me[0] * rows
    totals[...] = jnp.zeros_like(totals)
    part = 64

    def chunk(i, done):
        at = pl.ds(pl.multiple_of(i * part, part), part)
        there = pl.ds(pl.multiple_of(base + i * part, part), part)
        b = own[at, :] + peer1[at, :] + peer2[at, :] + peer3[at, :]
        v = volume[there, :].astype(F32)
        t = cotangent[there, :]

        def channel(c, carry):
            p0, p1 = carry
            w0, w1 = w_in[c, 0], w_in[c, 1]
            h = w0 * v + w1 * b + w_bias[c]
            gate = sigmoid(h)
            act = h * gate
            err = (w_out[c] * t) * (gate + act * (1.0 - gate))

            def fold(x):
                return jnp.sum(x.reshape(part // 8, 8, size), axis=0)

            totals[c, 0] += fold(err * v)
            totals[c, 1] += fold(err * b)
            totals[c, 2] += fold(err)
            totals[c, 3] += fold(act * t)
            return p0 + w0 * err, p1 + w1 * err

        zero = jnp.zeros_like(t)
        p0, p1 = lax.fori_loop(0, w_bias.shape[0], channel, (zero, zero), unroll=2)
        back_grad[at, :] = p1.astype(BF16)
        direct[at, :] = t + p0
        return done

    lax.fori_loop(0, rows // part, chunk, 0)
    for k in range(4):
        lanes = jnp.sum(totals[:, k], axis=1)
        sums[k : k + 1, :] = jnp.sum(lanes.T, axis=0, keepdims=True)


def call(body, out_shapes, specs, args, scratch=(), flops=0, bytes_moved=0, limit=56):
    return pl.pallas_call(
        body,
        out_shape=out_shapes,
        in_specs=specs,
        out_specs=[VMEM] * len(out_shapes),
        scratch_shapes=list(scratch),
        compiler_params=pltpu.CompilerParams(vmem_limit_bytes=limit * MIB),
        cost_estimate=pl.CostEstimate(
            flops=flops, bytes_accessed=bytes_moved, transcendentals=0
        ),
    )(*args)


def local(
    volume, dual, counts, cotangent, dual_in, dual_bias, dual_out,
    primal_in, primal_bias, primal_out, blocks, block_ray, block_vox, block_count,
):
    listed, tr, tv = blocks.shape[2:]
    voxels = volume.shape[1]
    tiles = voxels // tv
    views, det_rows, cols = dual.shape
    col_tiles = cols // tr
    ray_tiles = dual.size // tr
    channels = dual_bias.shape[0]
    groups = lax.axis_size("vert")
    slabs = lax.axis_size("gz")
    rows = tiles // groups
    me = lax.axis_index("vert").reshape(1).astype(jnp.int32)
    ray_total = 1.0 / (dual.size * slabs * groups)
    vox_total = 1.0 / (voxels * slabs)
    up = [(i, i + 1) for i in range(slabs - 1)]
    down = [(i + 1, i) for i in range(slabs - 1)]

    def shape(*dims, dtype=F32):
        return jax.ShapeDtypeStruct(dims, dtype)

    def beside(x):
        return lax.ppermute(x, "gz", up), lax.ppermute(x, "gz", down)

    def peer(x, d):
        return lax.ppermute(x, "vert", [(i, i ^ d) for i in range(groups)])

    def to_tiles(x):
        x = x.reshape(views, det_rows, col_tiles, tr).transpose(0, 2, 1, 3)
        return x.reshape(ray_tiles, tr)

    def from_tiles(x):
        x = x.reshape(views, col_tiles, det_rows, tr).transpose(0, 2, 1, 3)
        return x.reshape(views, det_rows, cols)

    matrix = blocks.reshape(listed * tr, tv)

    def in_vmem(after):
        held = call(
            hold_kernel,
            [pltpu.VMEM(matrix.shape, BF16)],
            [HBM, HBM],
            (pltpu.with_memory_space_constraint(matrix, pltpu.HBM), after),
            [pltpu.SemaphoreType.DMA((CHUNKS,))],
            bytes_moved=4 * matrix.size,
            limit=12,
        )[0]
        return pltpu.with_memory_space_constraint(held, pltpu.VMEM)

    count = block_count.reshape(1)
    vox = block_vox.reshape(listed)
    ray = block_ray.reshape(1, listed)
    per_view = det_rows * col_tiles
    ray = (ray // per_view) * per_view + (ray % col_tiles) * det_rows + (ray // col_tiles) % det_rows
    listed_at = lax.broadcasted_iota(jnp.int32, (1, listed), 1)
    vox_row = jnp.where(listed_at < count[0], vox[None, :], -1)
    field = volume.reshape(tiles, tv)
    cot = cotangent.reshape(tiles, tv)
    dual_tiles = to_tiles(dual)
    count_tiles = to_tiles(counts)

    big = [
        pltpu.VMEM((3 * tiles, tv), F32),
        pltpu.VMEM((listed, tv), F32),
        pltpu.VMEM((listed, tr), F32),
    ]
    low, high = beside(field)
    sinogram, partial = call(
        forward_kernel,
        [shape(ray_tiles, tr), shape(listed + 8, tv)],
        [SMEM] * 2 + [VMEM] * 8 + [SMEM] * 3,
        (count, vox, vox_row, ray, low, field, high, in_vmem(block_count), dual_tiles, count_tiles,
         dual_in, dual_bias, dual_out),
        big,
        bytes_moved=3 * matrix.size,
        limit=12,
    )

    def reduced(partial, sums):
        from_low, from_high = beside(partial)
        held, sums = call(
            own_kernel,
            [shape(groups, rows, tv), shape(*sums.shape)],
            [SMEM, VMEM, VMEM],
            (me, partial, sums),
            bytes_moved=4 * MIB,
            limit=16,
        )
        parts = call(
            fold_kernel,
            [shape(rows, tv)] * groups,
            [SMEM] + [VMEM] * 3,
            (me, held, from_low, from_high),
            bytes_moved=8 * MIB,
            limit=16,
        )
        return [parts[0]] + [peer(parts[d], d) for d in range(1, groups)], sums

    pieces, _ = reduced(partial, dual_bias)
    back_grad, direct, primal_sums = call(
        primal_kernel,
        [shape(rows, tv, dtype=BF16), shape(rows, tv), shape(4, channels)],
        [SMEM] + [VMEM] * 6 + [SMEM] * 3,
        (me, *pieces, field, cot, primal_in, primal_bias, primal_out),
        [pltpu.VMEM((channels, 4, 8, tv), F32)],
        bytes_moved=16 * MIB,
        limit=16,
    )
    near_low, near_high = beside(back_grad)
    near = jnp.stack([near_low, near_high])
    fields = [near_low, near_high, back_grad]
    for d in range(1, groups):
        fields += [peer(near, d), peer(back_grad, d)]
    grad_dual, partial, dual_sums = call(
        backward_kernel,
        [shape(ray_tiles, tr), shape(listed + 8, tv), shape(5, channels)],
        [SMEM] * 3 + [VMEM] * 15 + [SMEM] * 3,
        (me, count, vox, vox_row, ray, *fields, in_vmem(near), dual_tiles, count_tiles, sinogram,
         dual_in, dual_bias, dual_out),
        big + [pltpu.VMEM((channels, 5, 8, tr), F32)],
        bytes_moved=3 * matrix.size,
        limit=12,
    )
    sums = jnp.concatenate([dual_sums * ray_total, primal_sums * vox_total])
    pieces, sums = reduced(partial, sums)
    grad_volume = pieces[0] + pieces[1] + pieces[2] + pieces[3] + direct

    sent = jnp.broadcast_to(sums[None], (slabs * groups, *sums.shape))
    summed = jnp.sum(lax.all_to_all(sent, ("gz", "vert"), 0, 0), axis=0)
    return (
        grad_volume.reshape(1, rows * tv),
        from_tiles(grad_dual),
        summed[0:3].T,
        summed[3],
        summed[4],
        summed[5:7].T,
        summed[7],
        summed[8],
    )


def solution(mesh):
    in_specs = (
        P("gz", None),
        P("vert", "gz", None),
        P("vert", "gz", None),
        P("gz", None),
        P(), P(), P(), P(), P(), P(),
        P("gz", "vert", None, None, None),
        P("gz", "vert", None),
        P("gz", "vert", None),
        P("gz", "vert"),
    )
    out_specs = (P("gz", "vert"), P("vert", "gz", None), P(), P(), P(), P(), P(), P())
    return jax.shard_map(local, mesh=mesh, in_specs=in_specs, out_specs=out_specs, check_vma=False)
```

```python
import functools

import jax
import jax.numpy as jnp
from jax import lax
from jax.experimental import pallas as pl
from jax.experimental.pallas import tpu as pltpu
from jax.sharding import PartitionSpec as P

F32 = jnp.float32
BF16 = jnp.bfloat16
VMEM = pl.BlockSpec(memory_space=pltpu.VMEM)
SMEM = pl.BlockSpec(memory_space=pltpu.SMEM)
HBM = pl.BlockSpec(memory_space=pl.ANY)
NT = (((1,), (1,)), ((), ()))
GROUP = 16
CHUNKS = 16
MIB = 1024 * 1024


def sigmoid(x):
    return 0.5 * jnp.tanh(0.5 * x) + 0.5


def in_three(x):
    high = x.astype(BF16)
    rest = x - high.astype(F32)
    middle = rest.astype(BF16)
    return high, middle, (rest - middle.astype(F32)).astype(BF16)


def dot(a, b):
    return jnp.dot(a, b, preferred_element_type=F32)


def hold_kernel(blocks, _, held, sems):
    per = held.shape[0] // CHUNKS
    copies = []
    for i in range(CHUNKS):
        rows = pl.ds(i * per, per)
        copies.append(pltpu.make_async_copy(blocks.at[rows, :], held.at[rows, :], sems.at[i]))
        copies[i].start()
    for copy in copies:
        copy.wait()


def gather_tiles(vox, ext, picked):
    def body(i, carry):
        for j in range(16):
            b = i * 16 + j
            picked[pl.ds(b, 1), :] = ext[pl.ds(vox[b], 1), :]
        return carry

    lax.fori_loop(0, picked.shape[0] // 16, body, 0)


def project(held, picked, products):
    count, size = picked.shape
    row = lax.broadcasted_iota(jnp.int32, (GROUP, size), 0)
    for g in range(count // GROUP):
        x = picked[g * GROUP : (g + 1) * GROUP, :].astype(BF16)
        full = lax.dot_general(
            x,
            held[g * GROUP * size : (g + 1) * GROUP * size, :],
            NT,
            preferred_element_type=F32,
        )
        y = full[:, :size]
        for b in range(1, GROUP):
            y = jnp.where(row == b, full[:, b * size : (b + 1) * size], y)
        products[g * GROUP : (g + 1) * GROUP, :] = y


def spread(held, picked, out):
    count, size = picked.shape
    row = lax.broadcasted_iota(jnp.int32, (GROUP, size), 0)
    for g in range(count // GROUP):
        s = picked[g * GROUP : (g + 1) * GROUP, :]
        diagonal = jnp.concatenate(
            [jnp.where(row == b, s, 0.0).astype(BF16) for b in range(GROUP)], axis=1
        )
        out[g * GROUP : (g + 1) * GROUP, :] = dot(
            diagonal, held[g * GROUP * size : (g + 1) * GROUP * size, :]
        )


def mark_tiles(tile, out):
    count, size = tile.shape[1], out.shape[1]
    parts = [tile[:, i * size : (i + 1) * size] for i in range(count // size)]
    rows = jnp.concatenate(parts + parts, axis=0)
    out[count : count + 8, :] = rows.astype(F32)


def ray_choice(ray, count, tiles):
    shape = (tiles, ray.shape[1])
    tile = lax.broadcasted_iota(jnp.int32, shape, 0)
    block = lax.broadcasted_iota(jnp.int32, shape, 1)
    return jnp.where((ray[...] == tile) & (block < count[0]), 1.0, 0.0)


def add_rays(chosen, products):
    chosen = chosen.astype(BF16)
    high, middle, low = in_three(products[...])
    return dot(chosen, high) + dot(chosen, middle) + dot(chosen, low)


def forward_kernel(
    count, vox, tile, ray, low, own, high, blocks, dual, counts, w_in, w_bias, w_out,
    sinogram, partial, ext, picked, products,
):
    rows = own.shape[0]
    for i, field in enumerate((low, own, high)):
        ext[i * rows : (i + 1) * rows, :] = field[...].astype(F32)
    gather_tiles(vox, ext, picked)
    project(blocks, picked, products)
    tiles, size = dual.shape
    chosen = ray_choice(ray, count, tiles)
    sinogram[...] = add_rays(chosen, products)
    part = 64
    fresh = []
    for start in range(0, tiles, part):
        rows = slice(start, start + part)
        d = dual[rows, :]
        s = sinogram[rows, :]
        r = jnp.exp(-s) - counts[rows, :]

        def channel(c, total):
            h = w_in[c, 0] * d + w_in[c, 1] * s + w_in[c, 2] * r + w_bias[c]
            return total + w_out[c] * (h * sigmoid(h))

        fresh.append(lax.fori_loop(0, w_bias.shape[0], channel, jnp.zeros_like(d), unroll=4) + d)
    new_dual = jnp.concatenate(fresh, axis=0).astype(BF16)
    picked[...] = dot(chosen.T.astype(BF16), new_dual)
    spread(blocks, picked, partial)
    mark_tiles(tile, partial)


def backward_kernel(
    me, count, vox, tile, ray, low, high, own, near1, own1, near2, own2, near3, own3,
    blocks, dual, counts, sinogram, w_in, w_bias, w_out,
    grad_dual, partial, dual_grad, ext, picked, products,
):
    rows = own.shape[0]
    pieces = [
        (low, own, high),
        (near1.at[0], own1, near1.at[1]),
        (near2.at[0], own2, near2.at[1]),
        (near3.at[0], own3, near3.at[1]),
    ]
    for d, fields in enumerate(pieces):
        for i, field in enumerate(fields):
            at = pl.multiple_of((i * len(pieces) + (me[0] ^ d)) * rows, rows)
            ext[pl.ds(at, rows), :] = field[...].astype(F32)
    gather_tiles(vox, ext, picked)
    project(blocks, picked, products)
    tiles, size = dual.shape
    chosen = ray_choice(ray, count, tiles)
    dual_grad[...] = add_rays(chosen, products)
    part = 64
    grads = []
    for start in range(0, tiles, part):
        rows = slice(start, start + part)
        d = dual[rows, :]
        s = sinogram[rows, :]
        e = jnp.exp(-s)
        r = e - counts[rows, :]

        def channel(c, carry):
            p0, p1, p2 = carry
            w0, w1, w2 = w_in[c, 0], w_in[c, 1], w_in[c, 2]
            h = w0 * d + w1 * s + w2 * r + w_bias[c]
            gate = sigmoid(h)
            slope = gate + h * gate * (1.0 - gate)
            return p0 + (w0 * w_out[c]) * slope, p1 + (w1 * w_out[c]) * slope, p2 + (w2 * w_out[c]) * slope

        zero = jnp.zeros_like(d)
        p0, p1, p2 = lax.fori_loop(0, w_bias.shape[0], channel, (zero, zero, zero), unroll=4)
        g = dual_grad[rows, :]
        grad_dual[rows, :] = g + g * p0
        grads.append(g * (p1 - e * p2))
    sino_grad = jnp.concatenate(grads, axis=0).astype(BF16)
    picked[...] = dot(chosen.T.astype(BF16), sino_grad)
    spread(blocks, picked, partial)
    mark_tiles(tile, partial)


def weight_kernel(dual, counts, sinogram, dual_grad, w_in, w_bias, w_out, sums, totals):
    tiles, size = dual.shape
    totals[...] = jnp.zeros_like(totals)
    part = 64
    for start in range(0, tiles, part):
        rows = slice(start, start + part)
        d = dual[rows, :]
        s = sinogram[rows, :]
        r = jnp.exp(-s) - counts[rows, :]
        g = dual_grad[rows, :]

        def channel(c, done):
            h = w_in[c, 0] * d + w_in[c, 1] * s + w_in[c, 2] * r + w_bias[c]
            gate = sigmoid(h)
            act = h * gate
            err = (w_out[c] * g) * (gate + act * (1.0 - gate))

            def fold(x):
                return jnp.sum(x.reshape(part // 8, 8, size), axis=0)

            totals[c, 0] += fold(err * d)
            totals[c, 1] += fold(err * s)
            totals[c, 2] += fold(err * r)
            totals[c, 3] += fold(err)
            totals[c, 4] += fold(act * g)
            return done

        lax.fori_loop(0, w_bias.shape[0], channel, 0, unroll=2)
    for k in range(5):
        lanes = jnp.sum(totals[:, k], axis=1)
        sums[k : k + 1, :] = jnp.sum(lanes.T, axis=0, keepdims=True)


def final_kernel(own, peer1, peer2, peer3, direct, parts, *outs):
    outs[0][...] = own[...] + peer1[...] + peer2[...] + peer3[...] + direct[...]
    total = jnp.sum(parts[...], axis=0, keepdims=True)
    at = 0
    for out in outs[1:]:
        count, channels = out.shape
        for k in range(count):
            out[k : k + 1, :] = total[:, at : at + channels]
            at += channels


def split_marked(marked):
    count = marked.shape[0] - 8
    marks = marked[count:, :].astype(jnp.int32)
    vox = jnp.concatenate([marks[i : i + 1, :] for i in range(count // marked.shape[1])], axis=1)
    return vox, jnp.concatenate(in_three(marked[:count, :]), axis=1)


def place(vox, values, first, rows):
    tile = lax.broadcasted_iota(jnp.int32, (rows, vox.shape[1]), 0)
    chosen = jnp.where(vox - first == tile, 1.0, 0.0).astype(BF16)
    size = values.shape[1] // 3
    out = dot(chosen, values)
    return out[:, :size] + out[:, size : 2 * size] + out[:, 2 * size :]


def own_kernel(me, partial, out):
    groups, rows, _ = out.shape
    vox, values = split_marked(partial)
    for d in range(groups):
        out[d] = place(vox, values, (groups + (me[0] ^ d)) * rows, rows)


def fold_kernel(me, held, from_low, from_high, *outs):
    groups, rows, _ = held.shape
    vox_low, low = split_marked(from_low)
    vox_high, high = split_marked(from_high)
    for d in range(groups):
        first = (me[0] ^ d) * rows
        outs[d][...] = (
            held[d]
            + place(vox_low, low, 2 * groups * rows + first, rows)
            + place(vox_high, high, first, rows)
        )


def primal_kernel(
    me, own, peer1, peer2, peer3, volume, cotangent, w_in, w_bias, w_out,
    back_grad, direct, sums, totals,
):
    rows, size = own.shape
    base = me[0] * rows
    totals[...] = jnp.zeros_like(totals)
    part = 64

    def chunk(i, done):
        at = pl.ds(pl.multiple_of(i * part, part), part)
        there = pl.ds(pl.multiple_of(base + i * part, part), part)
        b = own[at, :] + peer1[at, :] + peer2[at, :] + peer3[at, :]
        v = volume[there, :].astype(F32)
        t = cotangent[there, :]

        def channel(c, carry):
            p0, p1 = carry
            w0, w1 = w_in[c, 0], w_in[c, 1]
            h = w0 * v + w1 * b + w_bias[c]
            gate = sigmoid(h)
            act = h * gate
            err = (w_out[c] * t) * (gate + act * (1.0 - gate))

            def fold(x):
                return jnp.sum(x.reshape(part // 8, 8, size), axis=0)

            totals[c, 0] += fold(err * v)
            totals[c, 1] += fold(err * b)
            totals[c, 2] += fold(err)
            totals[c, 3] += fold(act * t)
            return p0 + w0 * err, p1 + w1 * err

        zero = jnp.zeros_like(t)
        p0, p1 = lax.fori_loop(0, w_bias.shape[0], channel, (zero, zero), unroll=2)
        back_grad[at, :] = p1.astype(BF16)
        direct[at, :] = t + p0
        return done

    lax.fori_loop(0, rows // part, chunk, 0)
    for k in range(4):
        lanes = jnp.sum(totals[:, k], axis=1)
        sums[k : k + 1, :] = jnp.sum(lanes.T, axis=0, keepdims=True)


def call(body, out_shapes, specs, args, scratch=(), flops=0, bytes_moved=0, limit=56):
    return pl.pallas_call(
        body,
        out_shape=out_shapes,
        in_specs=specs,
        out_specs=[VMEM] * len(out_shapes),
        scratch_shapes=list(scratch),
        compiler_params=pltpu.CompilerParams(vmem_limit_bytes=limit * MIB),
        cost_estimate=pl.CostEstimate(
            flops=flops, bytes_accessed=bytes_moved, transcendentals=0
        ),
    )(*args)


def local(
    volume, dual, counts, cotangent, dual_in, dual_bias, dual_out,
    primal_in, primal_bias, primal_out, blocks, block_ray, block_vox, block_count,
):
    listed, tr, tv = blocks.shape[2:]
    voxels = volume.shape[1]
    tiles = voxels // tv
    views, det_rows, cols = dual.shape
    col_tiles = cols // tr
    ray_tiles = dual.size // tr
    channels = dual_bias.shape[0]
    groups = lax.axis_size("vert")
    slabs = lax.axis_size("gz")
    rows = tiles // groups
    me = lax.axis_index("vert").reshape(1).astype(jnp.int32)
    ray_total = 1.0 / (dual.size * slabs * groups)
    vox_total = 1.0 / (voxels * slabs)
    up = [(i, i + 1) for i in range(slabs - 1)]
    down = [(i + 1, i) for i in range(slabs - 1)]

    def shape(*dims, dtype=F32):
        return jax.ShapeDtypeStruct(dims, dtype)

    def beside(x):
        return lax.ppermute(x, "gz", up), lax.ppermute(x, "gz", down)

    def peer(x, d):
        return lax.ppermute(x, "vert", [(i, i ^ d) for i in range(groups)])

    def to_tiles(x):
        x = x.reshape(views, det_rows, col_tiles, tr).transpose(0, 2, 1, 3)
        return x.reshape(ray_tiles, tr)

    def from_tiles(x):
        x = x.reshape(views, col_tiles, det_rows, tr).transpose(0, 2, 1, 3)
        return x.reshape(views, det_rows, cols)

    matrix = blocks.reshape(listed * tr, tv)

    def in_vmem(after):
        held = call(
            hold_kernel,
            [pltpu.VMEM(matrix.shape, BF16)],
            [HBM, HBM],
            (pltpu.with_memory_space_constraint(matrix, pltpu.HBM), after),
            [pltpu.SemaphoreType.DMA((CHUNKS,))],
            bytes_moved=4 * matrix.size,
            limit=12,
        )[0]
        return pltpu.with_memory_space_constraint(held, pltpu.VMEM)

    count = block_count.reshape(1)
    vox = block_vox.reshape(listed)
    ray = block_ray.reshape(1, listed)
    per_view = det_rows * col_tiles
    ray = (ray // per_view) * per_view + (ray % col_tiles) * det_rows + (ray // col_tiles) % det_rows
    listed_at = lax.broadcasted_iota(jnp.int32, (1, listed), 1)
    vox_row = jnp.where(listed_at < count[0], vox[None, :], -1)
    field = volume.reshape(tiles, tv)
    cot = cotangent.reshape(tiles, tv)
    dual_tiles = to_tiles(dual)
    count_tiles = to_tiles(counts)

    big = [
        pltpu.VMEM((3 * tiles, tv), F32),
        pltpu.VMEM((listed, tv), F32),
        pltpu.VMEM((listed, tr), F32),
    ]
    low, high = beside(field)
    sinogram, partial = call(
        forward_kernel,
        [shape(ray_tiles, tr), shape(listed + 8, tv)],
        [SMEM] * 2 + [VMEM] * 8 + [SMEM] * 3,
        (count, vox, vox_row, ray, low, field, high, in_vmem(block_count), dual_tiles, count_tiles,
         dual_in, dual_bias, dual_out),
        big,
        bytes_moved=3 * matrix.size,
        limit=12,
    )

    def reduced(partial):
        from_low, from_high = beside(partial)
        held = call(
            own_kernel,
            [shape(groups, rows, tv)],
            [SMEM, VMEM],
            (me, partial),
            bytes_moved=4 * MIB,
            limit=16,
        )[0]
        parts = call(
            fold_kernel,
            [shape(rows, tv)] * groups,
            [SMEM] + [VMEM] * 3,
            (me, held, from_low, from_high),
            bytes_moved=8 * MIB,
            limit=16,
        )
        return [parts[0]] + [peer(parts[d], d) for d in range(1, groups)]

    pieces = reduced(partial)
    back_grad, direct, primal_sums = call(
        primal_kernel,
        [shape(rows, tv, dtype=BF16), shape(rows, tv), shape(4, channels)],
        [SMEM] + [VMEM] * 6 + [SMEM] * 3,
        (me, *pieces, field, cot, primal_in, primal_bias, primal_out),
        [pltpu.VMEM((channels, 4, 8, tv), F32)],
        bytes_moved=16 * MIB,
        limit=16,
    )
    near_low, near_high = beside(back_grad)
    near = jnp.stack([near_low, near_high])
    fields = [near_low, near_high, back_grad]
    for d in range(1, groups):
        fields += [peer(near, d), peer(back_grad, d)]
    grad_dual, partial, dual_grad = call(
        backward_kernel,
        [shape(ray_tiles, tr), shape(listed + 8, tv), shape(ray_tiles, tr)],
        [SMEM] * 3 + [VMEM] * 15 + [SMEM] * 3,
        (me, count, vox, vox_row, ray, *fields, in_vmem(near), dual_tiles, count_tiles, sinogram,
         dual_in, dual_bias, dual_out),
        big,
        bytes_moved=3 * matrix.size,
        limit=12,
    )
    dual_sums = call(
        weight_kernel,
        [shape(5, channels)],
        [VMEM] * 4 + [SMEM] * 3,
        (dual_tiles, count_tiles, sinogram, dual_grad, dual_in, dual_bias, dual_out),
        [pltpu.VMEM((channels, 5, 8, tr), F32)],
        bytes_moved=12 * MIB,
        limit=12,
    )[0]
    sums = jnp.concatenate([dual_sums * ray_total, primal_sums * vox_total])
    pieces = reduced(partial)
    dual_sums = call(
        weight_kernel,
        [shape(5, channels)],
        [VMEM] * 4 + [SMEM] * 3,
        (dual_tiles, count_tiles, sinogram, dual_grad, dual_in, dual_bias, dual_out),
        [pltpu.VMEM((channels, 5, 8, tr), F32)],
        bytes_moved=12 * MIB,
        limit=12,
    )[0]
    sums = jnp.concatenate([dual_sums * ray_total, primal_sums * vox_total])
    pieces = reduced(partial)
    grad_volume = pieces[0] + pieces[1] + pieces[2] + pieces[3] + direct

    sent = jnp.broadcast_to(sums.reshape(1, 1, -1), (slabs * groups, 1, sums.size))
    parts = lax.all_to_all(sent, ("gz", "vert"), 0, 0).reshape(slabs * groups, sums.size)
    widths = (dual_in.shape[1], 1, 1, primal_in.shape[1], 1, 1)
    grad_volume, *summed = call(
        final_kernel,
        [shape(rows, tv)] + [shape(width, channels) for width in widths],
        [VMEM] * 6,
        (*pieces, direct, parts),
        bytes_moved=4 * MIB,
        limit=12,
    )
    return (
        grad_volume.reshape(1, rows * tv),
        from_tiles(grad_dual),
        summed[0].T,
        summed[1].reshape(channels),
        summed[2].reshape(channels),
        summed[3].T,
        summed[4].reshape(channels),
        summed[5].reshape(channels),
    )


def solution(mesh):
    in_specs = (
        P("gz", None),
        P("vert", "gz", None),
        P("vert", "gz", None),
        P("gz", None),
        P(), P(), P(), P(), P(), P(),
        P("gz", "vert", None, None, None),
        P("gz", "vert", None),
        P("gz", "vert", None),
        P("gz", "vert"),
    )
    out_specs = (P("gz", "vert"), P("vert", "gz", None), P(), P(), P(), P(), P(), P())
    return jax.shard_map(local, mesh=mesh, in_specs=in_specs, out_specs=out_specs, check_vma=False)
```

```python
import functools

import jax
import jax.numpy as jnp
from jax import lax
from jax.experimental import pallas as pl
from jax.experimental.pallas import tpu as pltpu
from jax.sharding import PartitionSpec as P

F32 = jnp.float32
BF16 = jnp.bfloat16
VMEM = pl.BlockSpec(memory_space=pltpu.VMEM)
SMEM = pl.BlockSpec(memory_space=pltpu.SMEM)
HBM = pl.BlockSpec(memory_space=pl.ANY)
NT = (((1,), (1,)), ((), ()))
GROUP = 16
CHUNKS = 16
MIB = 1024 * 1024


def sigmoid(x):
    return 0.5 * jnp.tanh(0.5 * x) + 0.5


def in_three(x):
    high = x.astype(BF16)
    rest = x - high.astype(F32)
    middle = rest.astype(BF16)
    return high, middle, (rest - middle.astype(F32)).astype(BF16)


def dot(a, b):
    return jnp.dot(a, b, preferred_element_type=F32)


def start_copies(blocks, held, sems):
    per = held.shape[0] // CHUNKS
    copies = []
    for i in range(CHUNKS):
        rows = pl.ds(i * per, per)
        copies.append(pltpu.make_async_copy(blocks.at[rows, :], held.at[rows, :], sems.at[i]))
        copies[i].start()
    return copies


def hold_kernel(blocks, _, held, sems):
    for copy in start_copies(blocks, held, sems):
        copy.wait()


def gather_tiles(vox, ext, picked):
    def body(i, carry):
        for j in range(16):
            b = i * 16 + j
            picked[pl.ds(b, 1), :] = ext[pl.ds(vox[b], 1), :]
        return carry

    lax.fori_loop(0, picked.shape[0] // 16, body, 0)


def project(held, picked, products, copies=()):
    count, size = picked.shape
    row = lax.broadcasted_iota(jnp.int32, (GROUP, size), 0)
    groups = count // GROUP
    for g in range(groups):
        if copies and g % (groups // CHUNKS) == 0:
            copies[g // (groups // CHUNKS)].wait()
        x = picked[g * GROUP : (g + 1) * GROUP, :].astype(BF16)
        full = lax.dot_general(
            x,
            held[g * GROUP * size : (g + 1) * GROUP * size, :],
            NT,
            preferred_element_type=F32,
        )
        y = full[:, :size]
        for b in range(1, GROUP):
            y = jnp.where(row == b, full[:, b * size : (b + 1) * size], y)
        products[g * GROUP : (g + 1) * GROUP, :] = y


def spread(held, picked, out):
    count, size = picked.shape
    row = lax.broadcasted_iota(jnp.int32, (GROUP, size), 0)
    for g in range(count // GROUP):
        s = picked[g * GROUP : (g + 1) * GROUP, :]
        diagonal = jnp.concatenate(
            [jnp.where(row == b, s, 0.0).astype(BF16) for b in range(GROUP)], axis=1
        )
        out[g * GROUP : (g + 1) * GROUP, :] = dot(
            diagonal, held[g * GROUP * size : (g + 1) * GROUP * size, :]
        )


def mark_tiles(tile, out):
    count, size = tile.shape[1], out.shape[1]
    parts = [tile[:, i * size : (i + 1) * size] for i in range(count // size)]
    rows = jnp.concatenate(parts + parts, axis=0)
    out[count : count + 8, :] = rows.astype(F32)


def ray_choice(ray, count, tiles):
    shape = (tiles, ray.shape[1])
    tile = lax.broadcasted_iota(jnp.int32, shape, 0)
    block = lax.broadcasted_iota(jnp.int32, shape, 1)
    return jnp.where((ray[...] == tile) & (block < count[0]), 1.0, 0.0)


def add_rays(chosen, products):
    chosen = chosen.astype(BF16)
    high, middle, low = in_three(products[...])
    return dot(chosen, high) + dot(chosen, middle) + dot(chosen, low)


def forward_kernel(
    count, vox, tile, ray, low, own, high, blocks, dual, counts, w_in, w_bias, w_out,
    sinogram, partial, ext, picked, products,
):
    rows = own.shape[0]
    for i, field in enumerate((low, own, high)):
        ext[i * rows : (i + 1) * rows, :] = field[...].astype(F32)
    gather_tiles(vox, ext, picked)
    project(blocks, picked, products)
    tiles, size = dual.shape
    chosen = ray_choice(ray, count, tiles)
    sinogram[...] = add_rays(chosen, products)
    part = 64
    fresh = []
    for start in range(0, tiles, part):
        rows = slice(start, start + part)
        d = dual[rows, :]
        s = sinogram[rows, :]
        r = jnp.exp(-s) - counts[rows, :]

        def channel(c, total):
            h = w_in[c, 0] * d + w_in[c, 1] * s + w_in[c, 2] * r + w_bias[c]
            return total + w_out[c] * (h * sigmoid(h))

        fresh.append(lax.fori_loop(0, w_bias.shape[0], channel, jnp.zeros_like(d), unroll=4) + d)
    new_dual = jnp.concatenate(fresh, axis=0).astype(BF16)
    picked[...] = dot(chosen.T.astype(BF16), new_dual)
    spread(blocks, picked, partial)
    mark_tiles(tile, partial)


def backward_kernel(
    me, count, vox, tile, ray, low, high, own, near1, own1, near2, own2, near3, own3,
    blocks, dual, counts, sinogram, w_in, w_bias, w_out,
    grad_dual, partial, dual_grad, ext, picked, products, held, sems,
):
    copies = start_copies(blocks, held, sems)
    rows = own.shape[0]
    pieces = [
        (low, own, high),
        (near1.at[0], own1, near1.at[1]),
        (near2.at[0], own2, near2.at[1]),
        (near3.at[0], own3, near3.at[1]),
    ]
    for d, fields in enumerate(pieces):
        for i, field in enumerate(fields):
            at = pl.multiple_of((i * len(pieces) + (me[0] ^ d)) * rows, rows)
            ext[pl.ds(at, rows), :] = field[...].astype(F32)
    gather_tiles(vox, ext, picked)
    project(held, picked, products, copies)
    tiles, size = dual.shape
    chosen = ray_choice(ray, count, tiles)
    dual_grad[...] = add_rays(chosen, products)
    part = 64
    grads = []
    for start in range(0, tiles, part):
        rows = slice(start, start + part)
        d = dual[rows, :]
        s = sinogram[rows, :]
        e = jnp.exp(-s)
        r = e - counts[rows, :]

        def channel(c, carry):
            p0, p1, p2 = carry
            w0, w1, w2 = w_in[c, 0], w_in[c, 1], w_in[c, 2]
            h = w0 * d + w1 * s + w2 * r + w_bias[c]
            gate = sigmoid(h)
            slope = gate + h * gate * (1.0 - gate)
            return p0 + (w0 * w_out[c]) * slope, p1 + (w1 * w_out[c]) * slope, p2 + (w2 * w_out[c]) * slope

        zero = jnp.zeros_like(d)
        p0, p1, p2 = lax.fori_loop(0, w_bias.shape[0], channel, (zero, zero, zero), unroll=4)
        g = dual_grad[rows, :]
        grad_dual[rows, :] = g + g * p0
        grads.append(g * (p1 - e * p2))
    sino_grad = jnp.concatenate(grads, axis=0).astype(BF16)
    picked[...] = dot(chosen.T.astype(BF16), sino_grad)
    spread(held, picked, partial)
    mark_tiles(tile, partial)


def weight_kernel(dual, counts, sinogram, dual_grad, w_in, w_bias, w_out, sums, totals):
    tiles, size = dual.shape
    totals[...] = jnp.zeros_like(totals)
    part = 64
    for start in range(0, tiles, part):
        rows = slice(start, start + part)
        d = dual[rows, :]
        s = sinogram[rows, :]
        r = jnp.exp(-s) - counts[rows, :]
        g = dual_grad[rows, :]

        def channel(c, done):
            h = w_in[c, 0] * d + w_in[c, 1] * s + w_in[c, 2] * r + w_bias[c]
            gate = sigmoid(h)
            act = h * gate
            err = (w_out[c] * g) * (gate + act * (1.0 - gate))

            def fold(x):
                return jnp.sum(x.reshape(part // 8, 8, size), axis=0)

            totals[c, 0] += fold(err * d)
            totals[c, 1] += fold(err * s)
            totals[c, 2] += fold(err * r)
            totals[c, 3] += fold(err)
            totals[c, 4] += fold(act * g)
            return done

        lax.fori_loop(0, w_bias.shape[0], channel, 0, unroll=2)
    for k in range(5):
        lanes = jnp.sum(totals[:, k], axis=1)
        sums[k : k + 1, :] = jnp.sum(lanes.T, axis=0, keepdims=True)


def final_kernel(own, peer1, peer2, peer3, direct, parts, *outs):
    outs[0][...] = own[...] + peer1[...] + peer2[...] + peer3[...] + direct[...]
    total = jnp.sum(parts[...], axis=0, keepdims=True)
    at = 0
    for out in outs[1:]:
        count, channels = out.shape
        for k in range(count):
            out[k : k + 1, :] = total[:, at : at + channels]
            at += channels


def split_marked(marked):
    count = marked.shape[0] - 8
    marks = marked[count:, :].astype(jnp.int32)
    vox = jnp.concatenate([marks[i : i + 1, :] for i in range(count // marked.shape[1])], axis=1)
    return vox, jnp.concatenate(in_three(marked[:count, :]), axis=1)


def place(vox, values, first, rows):
    tile = lax.broadcasted_iota(jnp.int32, (rows, vox.shape[1]), 0)
    chosen = jnp.where(vox - first == tile, 1.0, 0.0).astype(BF16)
    size = values.shape[1] // 3
    out = dot(chosen, values)
    return out[:, :size] + out[:, size : 2 * size] + out[:, 2 * size :]


def own_kernel(me, partial, out):
    groups, rows, _ = out.shape
    vox, values = split_marked(partial)
    for d in range(groups):
        out[d] = place(vox, values, (groups + (me[0] ^ d)) * rows, rows)


def fold_kernel(me, held, from_low, from_high, *outs):
    groups, rows, _ = held.shape
    vox_low, low = split_marked(from_low)
    vox_high, high = split_marked(from_high)
    for d in range(groups):
        first = (me[0] ^ d) * rows
        outs[d][...] = (
            held[d]
            + place(vox_low, low, 2 * groups * rows + first, rows)
            + place(vox_high, high, first, rows)
        )


def primal_kernel(
    me, own, peer1, peer2, peer3, volume, cotangent, w_in, w_bias, w_out,
    back_grad, direct, sums, totals,
):
    rows, size = own.shape
    base = me[0] * rows
    totals[...] = jnp.zeros_like(totals)
    part = 64

    def chunk(i, done):
        at = pl.ds(pl.multiple_of(i * part, part), part)
        there = pl.ds(pl.multiple_of(base + i * part, part), part)
        b = own[at, :] + peer1[at, :] + peer2[at, :] + peer3[at, :]
        v = volume[there, :].astype(F32)
        t = cotangent[there, :]

        def channel(c, carry):
            p0, p1 = carry
            w0, w1, wo = w_in[c, 0], w_in[c, 1], 0.5 * w_out[c]
            half = (0.5 * w0) * v + ((0.5 * w1) * b + 0.5 * w_bias[c])
            more = jnp.tanh(half) + 1.0
            act = half * more
            err = t * (more * ((half - act) + (half + 1.0)))

            def fold(x):
                return jnp.sum(x.reshape(part // 8, 8, size), axis=0)

            totals[c, 0] += wo * fold(err * v)
            totals[c, 1] += wo * fold(err * b)
            totals[c, 2] += wo * fold(err)
            totals[c, 3] += fold(act * t)
            return p0 + (w0 * wo) * err, p1 + (w1 * wo) * err

        zero = jnp.zeros_like(t)
        p0, p1 = lax.fori_loop(0, w_bias.shape[0], channel, (zero, zero), unroll=2)
        back_grad[at, :] = p1.astype(BF16)
        direct[at, :] = t + p0
        return done

    lax.fori_loop(0, rows // part, chunk, 0)
    for k in range(4):
        lanes = jnp.sum(totals[:, k], axis=1)
        sums[k : k + 1, :] = jnp.sum(lanes.T, axis=0, keepdims=True)


def call(body, out_shapes, specs, args, scratch=(), flops=0, bytes_moved=0, limit=56):
    return pl.pallas_call(
        body,
        out_shape=out_shapes,
        in_specs=specs,
        out_specs=[VMEM] * len(out_shapes),
        scratch_shapes=list(scratch),
        compiler_params=pltpu.CompilerParams(vmem_limit_bytes=limit * MIB),
        cost_estimate=pl.CostEstimate(
            flops=flops, bytes_accessed=bytes_moved, transcendentals=0
        ),
    )(*args)


def local(
    volume, dual, counts, cotangent, dual_in, dual_bias, dual_out,
    primal_in, primal_bias, primal_out, blocks, block_ray, block_vox, block_count,
):
    listed, tr, tv = blocks.shape[2:]
    voxels = volume.shape[1]
    tiles = voxels // tv
    views, det_rows, cols = dual.shape
    col_tiles = cols // tr
    ray_tiles = dual.size // tr
    channels = dual_bias.shape[0]
    groups = lax.axis_size("vert")
    slabs = lax.axis_size("gz")
    rows = tiles // groups
    me = lax.axis_index("vert").reshape(1).astype(jnp.int32)
    ray_total = 1.0 / (dual.size * slabs * groups)
    vox_total = 1.0 / (voxels * slabs)
    up = [(i, i + 1) for i in range(slabs - 1)]
    down = [(i + 1, i) for i in range(slabs - 1)]

    def shape(*dims, dtype=F32):
        return jax.ShapeDtypeStruct(dims, dtype)

    def beside(x):
        return lax.ppermute(x, "gz", up), lax.ppermute(x, "gz", down)

    def peer(x, d):
        return lax.ppermute(x, "vert", [(i, i ^ d) for i in range(groups)])

    def to_tiles(x):
        x = x.reshape(views, det_rows, col_tiles, tr).transpose(0, 2, 1, 3)
        return x.reshape(ray_tiles, tr)

    def from_tiles(x):
        x = x.reshape(views, col_tiles, det_rows, tr).transpose(0, 2, 1, 3)
        return x.reshape(views, det_rows, cols)

    matrix = blocks.reshape(listed * tr, tv)

    in_hbm = pltpu.with_memory_space_constraint(matrix, pltpu.HBM)

    def in_vmem(after):
        held = call(
            hold_kernel,
            [pltpu.VMEM(matrix.shape, BF16)],
            [HBM, HBM],
            (in_hbm, after),
            [pltpu.SemaphoreType.DMA((CHUNKS,))],
            bytes_moved=4 * matrix.size,
            limit=12,
        )[0]
        return pltpu.with_memory_space_constraint(held, pltpu.VMEM)

    count = block_count.reshape(1)
    vox = block_vox.reshape(listed)
    ray = block_ray.reshape(1, listed)
    per_view = det_rows * col_tiles
    ray = (ray // per_view) * per_view + (ray % col_tiles) * det_rows + (ray // col_tiles) % det_rows
    listed_at = lax.broadcasted_iota(jnp.int32, (1, listed), 1)
    vox_row = jnp.where(listed_at < count[0], vox[None, :], -1)
    field = volume.reshape(tiles, tv)
    cot = cotangent.reshape(tiles, tv)
    dual_tiles = to_tiles(dual)
    count_tiles = to_tiles(counts)

    big = [
        pltpu.VMEM((3 * tiles, tv), F32),
        pltpu.VMEM((listed, tv), F32),
        pltpu.VMEM((listed, tr), F32),
    ]
    low, high = beside(field)
    sinogram, partial = call(
        forward_kernel,
        [shape(ray_tiles, tr), shape(listed + 8, tv)],
        [SMEM] * 2 + [VMEM] * 8 + [SMEM] * 3,
        (count, vox, vox_row, ray, low, field, high, in_vmem(block_count), dual_tiles, count_tiles,
         dual_in, dual_bias, dual_out),
        big,
        bytes_moved=3 * matrix.size,
        limit=12,
    )

    def reduced(partial):
        from_low, from_high = beside(partial)
        held = call(
            own_kernel,
            [shape(groups, rows, tv)],
            [SMEM, VMEM],
            (me, partial),
            bytes_moved=4 * MIB,
            limit=16,
        )[0]
        parts = call(
            fold_kernel,
            [shape(rows, tv)] * groups,
            [SMEM] + [VMEM] * 3,
            (me, held, from_low, from_high),
            bytes_moved=8 * MIB,
            limit=16,
        )
        return [parts[0]] + [peer(parts[d], d) for d in range(1, groups)]

    pieces = reduced(partial)
    back_grad, direct, primal_sums = call(
        primal_kernel,
        [shape(rows, tv, dtype=BF16), shape(rows, tv), shape(4, channels)],
        [SMEM] + [VMEM] * 6 + [SMEM] * 3,
        (me, *pieces, field, cot, primal_in, primal_bias, primal_out),
        [pltpu.VMEM((channels, 4, 8, tv), F32)],
        bytes_moved=16 * MIB,
        limit=16,
    )
    near_low, near_high = beside(back_grad)
    near = jnp.stack([near_low, near_high])
    fields = [near_low, near_high, back_grad]
    for d in range(1, groups):
        fields += [peer(near, d), peer(back_grad, d)]
    grad_dual, partial, dual_grad = call(
        backward_kernel,
        [shape(ray_tiles, tr), shape(listed + 8, tv), shape(ray_tiles, tr)],
        [SMEM] * 3 + [VMEM] * 11 + [HBM] + [VMEM] * 3 + [SMEM] * 3,
        (me, count, vox, vox_row, ray, *fields, in_hbm, dual_tiles, count_tiles, sinogram,
         dual_in, dual_bias, dual_out),
        big + [pltpu.VMEM(matrix.shape, BF16), pltpu.SemaphoreType.DMA((CHUNKS,))],
        bytes_moved=3 * matrix.size,
        limit=28,
    )
    dual_sums = call(
        weight_kernel,
        [shape(5, channels)],
        [VMEM] * 4 + [SMEM] * 3,
        (dual_tiles, count_tiles, sinogram, dual_grad, dual_in, dual_bias, dual_out),
        [pltpu.VMEM((channels, 5, 8, tr), F32)],
        bytes_moved=12 * MIB,
        limit=12,
    )[0]
    sums = jnp.concatenate([dual_sums * ray_total, primal_sums * vox_total])
    pieces = reduced(partial)
    dual_sums = call(
        weight_kernel,
        [shape(5, channels)],
        [VMEM] * 4 + [SMEM] * 3,
        (dual_tiles, count_tiles, sinogram, dual_grad, dual_in, dual_bias, dual_out),
        [pltpu.VMEM((channels, 5, 8, tr), F32)],
        bytes_moved=12 * MIB,
        limit=12,
    )[0]
    sums = jnp.concatenate([dual_sums * ray_total, primal_sums * vox_total])
    pieces = reduced(partial)
    grad_volume = pieces[0] + pieces[1] + pieces[2] + pieces[3] + direct

    sent = jnp.broadcast_to(sums.reshape(1, 1, -1), (slabs * groups, 1, sums.size))
    parts = lax.all_to_all(sent, ("gz", "vert"), 0, 0).reshape(slabs * groups, sums.size)
    widths = (dual_in.shape[1], 1, 1, primal_in.shape[1], 1, 1)
    grad_volume, *summed = call(
        final_kernel,
        [shape(rows, tv)] + [shape(width, channels) for width in widths],
        [VMEM] * 6,
        (*pieces, direct, parts),
        bytes_moved=4 * MIB,
        limit=12,
    )
    return (
        grad_volume.reshape(1, rows * tv),
        from_tiles(grad_dual),
        summed[0].T,
        summed[1].reshape(channels),
        summed[2].reshape(channels),
        summed[3].T,
        summed[4].reshape(channels),
        summed[5].reshape(channels),
    )


def solution(mesh):
    in_specs = (
        P("gz", None),
        P("vert", "gz", None),
        P("vert", "gz", None),
        P("gz", None),
        P(), P(), P(), P(), P(), P(),
        P("gz", "vert", None, None, None),
        P("gz", "vert", None),
        P("gz", "vert", None),
        P("gz", "vert"),
    )
    out_specs = (P("gz", "vert"), P("vert", "gz", None), P(), P(), P(), P(), P(), P())
    return jax.shard_map(local, mesh=mesh, in_specs=in_specs, out_specs=out_specs, check_vma=False)
```

```python
import functools

import jax
import jax.numpy as jnp
from jax import lax
from jax.experimental import pallas as pl
from jax.experimental.pallas import tpu as pltpu
from jax.sharding import PartitionSpec as P

F32 = jnp.float32
BF16 = jnp.bfloat16
VMEM = pl.BlockSpec(memory_space=pltpu.VMEM)
SMEM = pl.BlockSpec(memory_space=pltpu.SMEM)
HBM = pl.BlockSpec(memory_space=pl.ANY)
NT = (((1,), (1,)), ((), ()))
GROUP = 16
CHUNKS = 16
MIB = 1024 * 1024


def sigmoid(x):
    return 0.5 * jnp.tanh(0.5 * x) + 0.5


def in_three(x):
    high = x.astype(BF16)
    rest = x - high.astype(F32)
    middle = rest.astype(BF16)
    return high, middle, (rest - middle.astype(F32)).astype(BF16)


def dot(a, b):
    return jnp.dot(a, b, preferred_element_type=F32)


def start_copies(blocks, held, sems):
    per = held.shape[0] // CHUNKS
    copies = []
    for i in range(CHUNKS):
        rows = pl.ds(i * per, per)
        copies.append(pltpu.make_async_copy(blocks.at[rows, :], held.at[rows, :], sems.at[i]))
        copies[i].start()
    return copies


def hold_kernel(blocks, _, held, sems):
    for copy in start_copies(blocks, held, sems):
        copy.wait()


def gather_tiles(vox, ext, picked):
    def body(i, carry):
        for j in range(16):
            b = i * 16 + j
            picked[pl.ds(b, 1), :] = ext[pl.ds(vox[b], 1), :]
        return carry

    lax.fori_loop(0, picked.shape[0] // 16, body, 0)


def project(held, picked, products, copies=()):
    count, size = picked.shape
    row = lax.broadcasted_iota(jnp.int32, (GROUP, size), 0)
    groups = count // GROUP
    for g in range(groups):
        if copies and g % (groups // CHUNKS) == 0:
            copies[g // (groups // CHUNKS)].wait()
        x = picked[g * GROUP : (g + 1) * GROUP, :].astype(BF16)
        full = lax.dot_general(
            x,
            held[g * GROUP * size : (g + 1) * GROUP * size, :],
            NT,
            preferred_element_type=F32,
        )
        y = full[:, :size]
        for b in range(1, GROUP):
            y = jnp.where(row == b, full[:, b * size : (b + 1) * size], y)
        products[g * GROUP : (g + 1) * GROUP, :] = y


def spread(held, picked, out):
    count, size = picked.shape
    row = lax.broadcasted_iota(jnp.int32, (GROUP, size), 0)
    for g in range(count // GROUP):
        s = picked[g * GROUP : (g + 1) * GROUP, :]
        diagonal = jnp.concatenate(
            [jnp.where(row == b, s, 0.0).astype(BF16) for b in range(GROUP)], axis=1
        )
        out[g * GROUP : (g + 1) * GROUP, :] = dot(
            diagonal, held[g * GROUP * size : (g + 1) * GROUP * size, :]
        )


def mark_tiles(tile, out):
    count, size = tile.shape[1], out.shape[1]
    parts = [tile[:, i * size : (i + 1) * size] for i in range(count // size)]
    rows = jnp.concatenate(parts + parts, axis=0)
    out[count : count + 8, :] = rows.astype(F32)


def ray_choice(ray, count, tiles):
    shape = (tiles, ray.shape[1])
    tile = lax.broadcasted_iota(jnp.int32, shape, 0)
    block = lax.broadcasted_iota(jnp.int32, shape, 1)
    return jnp.where((ray[...] == tile) & (block < count[0]), 1.0, 0.0)


def add_rays(chosen, products):
    chosen = chosen.astype(BF16)
    high, middle, low = in_three(products[...])
    return dot(chosen, high) + dot(chosen, middle) + dot(chosen, low)


def forward_kernel(
    count, vox, tile, ray, low, own, high, blocks, dual, counts, w_in, w_bias, w_out,
    sinogram, partial, ext, picked, products,
):
    rows = own.shape[0]
    for i, field in enumerate((low, own, high)):
        ext[i * rows : (i + 1) * rows, :] = field[...].astype(F32)
    gather_tiles(vox, ext, picked)
    project(blocks, picked, products)
    tiles, size = dual.shape
    chosen = ray_choice(ray, count, tiles)
    sinogram[...] = add_rays(chosen, products)
    part = 64
    fresh = []
    for start in range(0, tiles, part):
        rows = slice(start, start + part)
        d = dual[rows, :]
        s = sinogram[rows, :]
        r = jnp.exp(-s) - counts[rows, :]

        def channel(c, total):
            h = w_in[c, 0] * d + w_in[c, 1] * s + w_in[c, 2] * r + w_bias[c]
            return total + w_out[c] * (h * sigmoid(h))

        fresh.append(lax.fori_loop(0, w_bias.shape[0], channel, jnp.zeros_like(d), unroll=4) + d)
    new_dual = jnp.concatenate(fresh, axis=0).astype(BF16)
    picked[...] = dot(chosen.T.astype(BF16), new_dual)
    spread(blocks, picked, partial)
    mark_tiles(tile, partial)


def backward_kernel(
    me, count, vox, tile, ray, low, high, own, near1, own1, near2, own2, near3, own3,
    blocks, dual, counts, sinogram, w_in, w_bias, w_out,
    grad_dual, partial, dual_grad, ext, picked, products, held, sems,
):
    copies = start_copies(blocks, held, sems)
    rows = own.shape[0]
    pieces = [
        (low, own, high),
        (near1.at[0], own1, near1.at[1]),
        (near2.at[0], own2, near2.at[1]),
        (near3.at[0], own3, near3.at[1]),
    ]
    for d, fields in enumerate(pieces):
        for i, field in enumerate(fields):
            at = pl.multiple_of((i * len(pieces) + (me[0] ^ d)) * rows, rows)
            ext[pl.ds(at, rows), :] = field[...].astype(F32)
    gather_tiles(vox, ext, picked)
    project(held, picked, products, copies)
    tiles, size = dual.shape
    chosen = ray_choice(ray, count, tiles)
    dual_grad[...] = add_rays(chosen, products)
    part = 64
    grads = []
    for start in range(0, tiles, part):
        rows = slice(start, start + part)
        d = dual[rows, :]
        s = sinogram[rows, :]
        e = jnp.exp(-s)
        r = e - counts[rows, :]

        def channel(c, carry):
            p0, p1, p2 = carry
            w0, w1, w2 = w_in[c, 0], w_in[c, 1], w_in[c, 2]
            h = w0 * d + w1 * s + w2 * r + w_bias[c]
            gate = sigmoid(h)
            slope = gate + h * gate * (1.0 - gate)
            return p0 + (w0 * w_out[c]) * slope, p1 + (w1 * w_out[c]) * slope, p2 + (w2 * w_out[c]) * slope

        zero = jnp.zeros_like(d)
        p0, p1, p2 = lax.fori_loop(0, w_bias.shape[0], channel, (zero, zero, zero), unroll=4)
        g = dual_grad[rows, :]
        grad_dual[rows, :] = g + g * p0
        grads.append(g * (p1 - e * p2))
    sino_grad = jnp.concatenate(grads, axis=0).astype(BF16)
    picked[...] = dot(chosen.T.astype(BF16), sino_grad)
    spread(held, picked, partial)
    mark_tiles(tile, partial)


def weight_kernel(dual, counts, sinogram, dual_grad, w_in, w_bias, w_out, sums, totals):
    tiles, size = dual.shape
    totals[...] = jnp.zeros_like(totals)
    part = 64
    for start in range(0, tiles, part):
        rows = slice(start, start + part)
        d = dual[rows, :]
        s = sinogram[rows, :]
        r = jnp.exp(-s) - counts[rows, :]
        g = dual_grad[rows, :]

        def channel(c, done):
            half = (0.5 * w_in[c, 0]) * d + (0.5 * w_in[c, 1]) * s
            half = half + ((0.5 * w_in[c, 2]) * r + 0.5 * w_bias[c])
            more = jnp.tanh(half) + 1.0
            act = half * more
            wo = 0.5 * w_out[c]
            err = g * (more * ((half - act) + (half + 1.0)))

            def fold(x):
                return jnp.sum(x.reshape(part // 8, 8, size), axis=0)

            totals[c, 0] += wo * fold(err * d)
            totals[c, 1] += wo * fold(err * s)
            totals[c, 2] += wo * fold(err * r)
            totals[c, 3] += wo * fold(err)
            totals[c, 4] += fold(act * g)
            return done

        lax.fori_loop(0, w_bias.shape[0], channel, 0, unroll=4)
    for k in range(5):
        lanes = jnp.sum(totals[:, k], axis=1)
        sums[k : k + 1, :] = jnp.sum(lanes.T, axis=0, keepdims=True)


def final_kernel(own, peer1, peer2, peer3, direct, parts, *outs):
    outs[0][...] = own[...] + peer1[...] + peer2[...] + peer3[...] + direct[...]
    total = jnp.sum(parts[...], axis=0, keepdims=True)
    at = 0
    for out in outs[1:]:
        count, channels = out.shape
        for k in range(count):
            out[k : k + 1, :] = total[:, at : at + channels]
            at += channels


def split_marked(marked):
    count = marked.shape[0] - 8
    marks = marked[count:, :].astype(jnp.int32)
    vox = jnp.concatenate([marks[i : i + 1, :] for i in range(count // marked.shape[1])], axis=1)
    return vox, jnp.concatenate(in_three(marked[:count, :]), axis=1)


def place(vox, values, first, rows):
    tile = lax.broadcasted_iota(jnp.int32, (rows, vox.shape[1]), 0)
    chosen = jnp.where(vox - first == tile, 1.0, 0.0).astype(BF16)
    size = values.shape[1] // 3
    out = dot(chosen, values)
    return out[:, :size] + out[:, size : 2 * size] + out[:, 2 * size :]


def own_kernel(me, partial, out):
    groups, rows, _ = out.shape
    vox, values = split_marked(partial)
    for d in range(groups):
        out[d] = place(vox, values, (groups + (me[0] ^ d)) * rows, rows)


def fold_kernel(me, held, from_low, from_high, *outs):
    groups, rows, _ = held.shape
    vox_low, low = split_marked(from_low)
    vox_high, high = split_marked(from_high)
    for d in range(groups):
        first = (me[0] ^ d) * rows
        outs[d][...] = (
            held[d]
            + place(vox_low, low, 2 * groups * rows + first, rows)
            + place(vox_high, high, first, rows)
        )


def primal_kernel(
    me, own, peer1, peer2, peer3, volume, cotangent, w_in, w_bias, w_out,
    back_grad, direct, sums, totals,
):
    rows, size = own.shape
    base = me[0] * rows
    totals[...] = jnp.zeros_like(totals)
    part = 64

    def chunk(i, done):
        at = pl.ds(pl.multiple_of(i * part, part), part)
        there = pl.ds(pl.multiple_of(base + i * part, part), part)
        b = own[at, :] + peer1[at, :] + peer2[at, :] + peer3[at, :]
        v = volume[there, :].astype(F32)
        t = cotangent[there, :]

        def channel(c, carry):
            p0, p1 = carry
            w0, w1, wo = w_in[c, 0], w_in[c, 1], 0.5 * w_out[c]
            half = (0.5 * w0) * v + ((0.5 * w1) * b + 0.5 * w_bias[c])
            more = jnp.tanh(half) + 1.0
            act = half * more
            err = t * (more * ((half - act) + (half + 1.0)))

            def fold(x):
                return jnp.sum(x.reshape(part // 8, 8, size), axis=0)

            totals[c, 0] += wo * fold(err * v)
            totals[c, 1] += wo * fold(err * b)
            totals[c, 2] += wo * fold(err)
            totals[c, 3] += fold(act * t)
            return p0 + (w0 * wo) * err, p1 + (w1 * wo) * err

        zero = jnp.zeros_like(t)
        p0, p1 = lax.fori_loop(0, w_bias.shape[0], channel, (zero, zero), unroll=2)
        back_grad[at, :] = p1.astype(BF16)
        direct[at, :] = t + p0
        return done

    lax.fori_loop(0, rows // part, chunk, 0)
    for k in range(4):
        lanes = jnp.sum(totals[:, k], axis=1)
        sums[k : k + 1, :] = jnp.sum(lanes.T, axis=0, keepdims=True)


def call(body, out_shapes, specs, args, scratch=(), flops=0, bytes_moved=0, limit=56):
    return pl.pallas_call(
        body,
        out_shape=out_shapes,
        in_specs=specs,
        out_specs=[VMEM] * len(out_shapes),
        scratch_shapes=list(scratch),
        compiler_params=pltpu.CompilerParams(vmem_limit_bytes=limit * MIB),
        cost_estimate=pl.CostEstimate(
            flops=flops, bytes_accessed=bytes_moved, transcendentals=0
        ),
    )(*args)


def local(
    volume, dual, counts, cotangent, dual_in, dual_bias, dual_out,
    primal_in, primal_bias, primal_out, blocks, block_ray, block_vox, block_count,
):
    listed, tr, tv = blocks.shape[2:]
    voxels = volume.shape[1]
    tiles = voxels // tv
    views, det_rows, cols = dual.shape
    col_tiles = cols // tr
    ray_tiles = dual.size // tr
    channels = dual_bias.shape[0]
    groups = lax.axis_size("vert")
    slabs = lax.axis_size("gz")
    rows = tiles // groups
    me = lax.axis_index("vert").reshape(1).astype(jnp.int32)
    ray_total = 1.0 / (dual.size * slabs * groups)
    vox_total = 1.0 / (voxels * slabs)
    up = [(i, i + 1) for i in range(slabs - 1)]
    down = [(i + 1, i) for i in range(slabs - 1)]

    def shape(*dims, dtype=F32):
        return jax.ShapeDtypeStruct(dims, dtype)

    def beside(x):
        return lax.ppermute(x, "gz", up), lax.ppermute(x, "gz", down)

    def peer(x, d):
        return lax.ppermute(x, "vert", [(i, i ^ d) for i in range(groups)])

    def to_tiles(x):
        x = x.reshape(views, det_rows, col_tiles, tr).transpose(0, 2, 1, 3)
        return x.reshape(ray_tiles, tr)

    def from_tiles(x):
        x = x.reshape(views, col_tiles, det_rows, tr).transpose(0, 2, 1, 3)
        return x.reshape(views, det_rows, cols)

    matrix = blocks.reshape(listed * tr, tv)

    in_hbm = pltpu.with_memory_space_constraint(matrix, pltpu.HBM)

    def in_vmem(after):
        held = call(
            hold_kernel,
            [pltpu.VMEM(matrix.shape, BF16)],
            [HBM, HBM],
            (in_hbm, after),
            [pltpu.SemaphoreType.DMA((CHUNKS,))],
            bytes_moved=4 * matrix.size,
            limit=12,
        )[0]
        return pltpu.with_memory_space_constraint(held, pltpu.VMEM)

    count = block_count.reshape(1)
    vox = block_vox.reshape(listed)
    ray = block_ray.reshape(1, listed)
    per_view = det_rows * col_tiles
    ray = (ray // per_view) * per_view + (ray % col_tiles) * det_rows + (ray // col_tiles) % det_rows
    listed_at = lax.broadcasted_iota(jnp.int32, (1, listed), 1)
    vox_row = jnp.where(listed_at < count[0], vox[None, :], -1)
    field = volume.reshape(tiles, tv)
    cot = cotangent.reshape(tiles, tv)
    dual_tiles = to_tiles(dual)
    count_tiles = to_tiles(counts)

    big = [
        pltpu.VMEM((3 * tiles, tv), F32),
        pltpu.VMEM((listed, tv), F32),
        pltpu.VMEM((listed, tr), F32),
    ]
    low, high = beside(field)
    sinogram, partial = call(
        forward_kernel,
        [shape(ray_tiles, tr), shape(listed + 8, tv)],
        [SMEM] * 2 + [VMEM] * 8 + [SMEM] * 3,
        (count, vox, vox_row, ray, low, field, high, in_vmem(block_count), dual_tiles, count_tiles,
         dual_in, dual_bias, dual_out),
        big,
        bytes_moved=3 * matrix.size,
        limit=12,
    )

    def reduced(partial):
        from_low, from_high = beside(partial)
        held = call(
            own_kernel,
            [shape(groups, rows, tv)],
            [SMEM, VMEM],
            (me, partial),
            bytes_moved=4 * MIB,
            limit=16,
        )[0]
        parts = call(
            fold_kernel,
            [shape(rows, tv)] * groups,
            [SMEM] + [VMEM] * 3,
            (me, held, from_low, from_high),
            bytes_moved=8 * MIB,
            limit=16,
        )
        return [parts[0]] + [peer(parts[d], d) for d in range(1, groups)]

    pieces = reduced(partial)
    back_grad, direct, primal_sums = call(
        primal_kernel,
        [shape(rows, tv, dtype=BF16), shape(rows, tv), shape(4, channels)],
        [SMEM] + [VMEM] * 6 + [SMEM] * 3,
        (me, *pieces, field, cot, primal_in, primal_bias, primal_out),
        [pltpu.VMEM((channels, 4, 8, tv), F32)],
        bytes_moved=16 * MIB,
        limit=16,
    )
    near_low, near_high = beside(back_grad)
    near = jnp.stack([near_low, near_high])
    fields = [near_low, near_high, back_grad]
    for d in range(1, groups):
        fields += [peer(near, d), peer(back_grad, d)]
    grad_dual, partial, dual_grad = call(
        backward_kernel,
        [shape(ray_tiles, tr), shape(listed + 8, tv), shape(ray_tiles, tr)],
        [SMEM] * 3 + [VMEM] * 11 + [HBM] + [VMEM] * 3 + [SMEM] * 3,
        (me, count, vox, vox_row, ray, *fields, in_hbm, dual_tiles, count_tiles, sinogram,
         dual_in, dual_bias, dual_out),
        big + [pltpu.VMEM(matrix.shape, BF16), pltpu.SemaphoreType.DMA((CHUNKS,))],
        bytes_moved=3 * matrix.size,
        limit=28,
    )
    dual_sums = call(
        weight_kernel,
        [shape(5, channels)],
        [VMEM] * 4 + [SMEM] * 3,
        (dual_tiles, count_tiles, sinogram, dual_grad, dual_in, dual_bias, dual_out),
        [pltpu.VMEM((channels, 5, 8, tr), F32)],
        bytes_moved=12 * MIB,
        limit=12,
    )[0]
    sums = jnp.concatenate([dual_sums * ray_total, primal_sums * vox_total])
    pieces = reduced(partial)
    dual_sums = call(
        weight_kernel,
        [shape(5, channels)],
        [VMEM] * 4 + [SMEM] * 3,
        (dual_tiles, count_tiles, sinogram, dual_grad, dual_in, dual_bias, dual_out),
        [pltpu.VMEM((channels, 5, 8, tr), F32)],
        bytes_moved=12 * MIB,
        limit=12,
    )[0]
    sums = jnp.concatenate([dual_sums * ray_total, primal_sums * vox_total])
    pieces = reduced(partial)
    grad_volume = pieces[0] + pieces[1] + pieces[2] + pieces[3] + direct

    sent = jnp.broadcast_to(sums.reshape(1, 1, -1), (slabs * groups, 1, sums.size))
    parts = lax.all_to_all(sent, ("gz", "vert"), 0, 0).reshape(slabs * groups, sums.size)
    widths = (dual_in.shape[1], 1, 1, primal_in.shape[1], 1, 1)
    grad_volume, *summed = call(
        final_kernel,
        [shape(rows, tv)] + [shape(width, channels) for width in widths],
        [VMEM] * 6,
        (*pieces, direct, parts),
        bytes_moved=4 * MIB,
        limit=12,
    )
    return (
        grad_volume.reshape(1, rows * tv),
        from_tiles(grad_dual),
        summed[0].T,
        summed[1].reshape(channels),
        summed[2].reshape(channels),
        summed[3].T,
        summed[4].reshape(channels),
        summed[5].reshape(channels),
    )


def solution(mesh):
    in_specs = (
        P("gz", None),
        P("vert", "gz", None),
        P("vert", "gz", None),
        P("gz", None),
        P(), P(), P(), P(), P(), P(),
        P("gz", "vert", None, None, None),
        P("gz", "vert", None),
        P("gz", "vert", None),
        P("gz", "vert"),
    )
    out_specs = (P("gz", "vert"), P("vert", "gz", None), P(), P(), P(), P(), P(), P())
    return jax.shard_map(local, mesh=mesh, in_specs=in_specs, out_specs=out_specs, check_vma=False)
```
